256 devices in a mesh: ctx: 16 (over x, z_hi, core), dp: 16 (over z_lo, y).
Axes of the slice: x: 4, y: 4, z: 8 (z_hi: 2, z_lo: 4; z = z_hi * 4 + z_lo), core: 2. Of those that a mesh axis runs over, the one named last changes fastest.
Arguments:
- query_proj: bfloat16 [16, 2048, 4096], P('dp', 'ctx'), may hold values from -6 to 6
- key_proj: bfloat16 [16, 2048, 4096], P('dp', 'ctx'), may hold values from -6 to 6
- value_proj: bfloat16 [16, 2048, 4096], P('dp', 'ctx'), may hold values from -6 to 6
- short_taps: float32 [3, 7, 4096], replicated, may hold values from -2.4 to 2.4
- filter_taps: float32 [256, 128], replicated, may hold values from -0.54 to 0.54
- skip_gain: float32 [4096], replicated, may hold values from -1 to 1
- doc_lengths: int32 [16, 8], P('dp'), may hold values from 1 to 1024, 2048 in all within a row
- out_grad: bfloat16 [16, 2048, 4096], P('dp', 'ctx'), may hold values from -6 to 6
Outputs:
- mixed: bfloat16 [16, 2048, 4096], P('dp', 'ctx')
- grad_query: bfloat16 [16, 2048, 4096], P('dp', 'ctx')
- grad_key: bfloat16 [16, 2048, 4096], P('dp', 'ctx')
- grad_value: bfloat16 [16, 2048, 4096], P('dp', 'ctx')
- grad_short: float32 [3, 7, 4096], replicated
- grad_filter: float32 [256, 128], replicated
- grad_skip: float32 [4096], replicated
The draws below stay inside these ranges and needn't reach their ends.
Inputs may be any that keep to these rules, and one draw needn't show every extreme that they name: `doc_lengths`: each row holds the lengths of the 8 documents of one context in order; they sum to 2048 and the longest is exactly half of 2048.
All inputs are finite; a program needn't handle non-finite values.
Results may differ from the reference program's by a relative error of at most 0.007.
Values may be sent and summed in bfloat16 or wider, within the bound.
A program may use at most 320 MiB of HBM per device.

```python
import math
import jax
import jax.numpy as jnp
import numpy as np
from jax import lax

CH = 4096
FEAT = 7
FILT = 128
NDOC = 8
GRP = 256
SEQ = 2048
GROUPS = 16


def levels(rng, dims, pieces, least, largest):
    loudness, own = 1.0, jax.random.fold_in(rng, 6)
    for dim, shards_of in pieces:
        draws = jnp.exp(jax.random.uniform(jax.random.fold_in(own, dim), (shards_of,), jnp.float32, least / len(pieces), largest / len(pieces)))
        loudness = loudness * jnp.repeat(draws, dims[dim] // shards_of).reshape([-1 if axis == dim else 1 for axis in range(len(dims))])
    return loudness


def split_up(number_of, total, most, lean):
    weights = [(1 << 20) // math.isqrt(standing ** lean) + 1 for standing in range(2, number_of + 1)]
    surplus, given = total - most - (number_of - 1), [1] * (number_of - 1)
    while surplus > 0:
        free = [i for i in range(number_of - 1) if given[i] < most]
        mass, remaining = sum([weights[i] for i in free]), surplus
        for i in free:
            extra = min(most - given[i], max(1, remaining * weights[i] // mass), surplus)
            given[i] = given[i] + extra
            surplus = surplus - extra
    return np.array([most] + given)


def uneven(key, count, total, limit, slope):
    if count == 2:
        one = jax.random.randint(key, (), max(1, total - limit), min(limit, total - 1) + 1)
        return jnp.stack([one, total - one])
    tallies = jnp.asarray(split_up(count, total, limit, slope), jnp.int32)
    pairs = (count - 1) // 2
    source_of, receiver = tallies[1:1 + 2 * pairs:2], tallies[2:2 + 2 * pairs:2]
    room = jnp.minimum(source_of - 1, limit - receiver)
    moved = jax.random.randint(jax.random.fold_in(key, 1), (pairs,), 0, 1 << 20) % (room + 1)
    tallies = tallies.at[1:1 + 2 * pairs:2].set(source_of - moved).at[2:2 + 2 * pairs:2].set(receiver + moved)
    return tallies[jax.random.permutation(jax.random.fold_in(key, 2), count)]


def bell_draw(own_key, shape, deviation, reach, shards=(), kind=jnp.bfloat16):
    values = jax.random.normal(own_key, shape, jnp.float32) * deviation
    if len(shards) > 0:
        values = levels(own_key, shape, shards, -0.22, 0.18) * values
    return jnp.clip(values, min=-reach, max=reach).astype(kind)


def setup_inputs(seed: int = 0) -> dict:
    key_list = jax.random.split(jax.random.key(seed), 9)
    query_proj = bell_draw(key_list[0], (GROUPS, SEQ, CH), 1.0, 6.0, ((0, 16), (1, 16)))
    key_proj = bell_draw(key_list[1], (GROUPS, SEQ, CH), 1.0, 6.0, ((0, 16), (1, 16)))
    value_proj = bell_draw(key_list[2], (GROUPS, SEQ, CH), 1.0, 6.0, ((0, 16), (1, 16)))
    short_taps = bell_draw(key_list[3], (3, FEAT, CH), 0.4, 2.4, (), jnp.float32)
    filter_taps = bell_draw(key_list[4], (GRP, FILT), 0.09, 0.54, (), jnp.float32)
    skip_gain = jnp.clip(jax.random.uniform(key_list[5], (CH,), jnp.float32, -1.0, 1.0), -1.0, 1.0)
    doc_lengths = jax.vmap(lambda own: uneven(own, NDOC, SEQ, SEQ // 2, 2))(jax.random.split(key_list[6], GROUPS)).reshape((GROUPS, NDOC)).astype(jnp.int32)
    out_grad = bell_draw(key_list[7], (GROUPS, SEQ, CH), 1.0, 6.0, ((0, 16), (1, 16)))
    return {"query_proj": query_proj, "key_proj": key_proj, "value_proj": value_proj, "short_taps": short_taps, "filter_taps": filter_taps, "skip_gain": skip_gain, "doc_lengths": doc_lengths, "out_grad": out_grad}


def toeplitz(taps):
    groups, length = taps.shape
    pattern = jnp.concatenate([jnp.zeros((groups, 1), taps.dtype), taps[:, ::-1], jnp.zeros((groups, length), taps.dtype)], axis=1)
    tiled = jnp.tile(pattern, (1, length))[:, :2 * length * length]
    return tiled.reshape(groups, length, 2 * length)

def doc_index(starts, positions):
    return lax.optimization_barrier(jnp.sum((positions[:, None] >= starts[None, :]).astype(jnp.int32), axis=1)) - 1

def featurize(extended, kernel, doc_window, number):
    margin = kernel.shape[0] - 1
    own_docs = doc_window[margin:]
    result = jnp.zeros((number, extended.shape[1]), jnp.float32)
    for offset in range(kernel.shape[0]):
        matches = (doc_window[margin - offset:margin - offset + number] == own_docs).astype(jnp.float32)
        result = result + kernel[offset][None, :] * extended[margin - offset:margin - offset + number] * matches[:, None]
    return result

def featurize_back(grad_window, kernel, doc_window, number):
    own_docs = doc_window[:number]
    result = jnp.zeros((number, grad_window.shape[1]), jnp.float32)
    for offset in range(kernel.shape[0]):
        matches = (doc_window[offset:offset + number] == own_docs).astype(jnp.float32)
        result = result + kernel[offset][None, :] * grad_window[offset:offset + number] * matches[:, None]
    return result

def tap_grads(gradient, extended, doc_window, number, count_taps):
    margin = count_taps - 1
    own_docs = doc_window[margin:]
    result = []
    for offset in range(count_taps):
        matches = (doc_window[margin - offset:margin - offset + number] == own_docs).astype(jnp.float32)
        result.append(lax.optimization_barrier(jnp.sum(gradient * extended[margin - offset:margin - offset + number] * matches[:, None], axis=0)))
    return jnp.stack(result)

def one_group(query, keys, values, cotangent, lengths, short_taps, filter_taps, skip_gain):
    seq, width = query.shape
    groups, filter_len = filter_taps.shape
    group_width = width // groups
    count_taps = short_taps.shape[1]
    margin = count_taps - 1
    starts = jnp.cumsum(lengths) - lengths
    base = filter_len + margin
    positions = jnp.arange(seq + 2 * filter_len + margin, dtype=jnp.int32) - base
    all_docs = doc_index(starts, positions)
    feat_docs = all_docs[filter_len:base + seq]
    blank = jnp.zeros((margin, width), jnp.float32)
    q_ext = jnp.concatenate([blank, query.astype(jnp.float32)], 0)
    k_ext = jnp.concatenate([blank, keys.astype(jnp.float32)], 0)
    v_ext = jnp.concatenate([blank, values.astype(jnp.float32)], 0)
    q_feat = featurize(q_ext, short_taps[0], feat_docs, seq)
    k_feat = featurize(k_ext, short_taps[1], feat_docs, seq)
    v_feat = featurize(v_ext, short_taps[2], feat_docs, seq)
    u_local = lax.optimization_barrier((k_feat * v_feat).astype(jnp.bfloat16))
    u_float = u_local.astype(jnp.float32)
    u_window = jnp.concatenate([jnp.zeros((filter_len, width), jnp.float32), u_float], 0)
    taps_b = lax.optimization_barrier(filter_taps.astype(jnp.bfloat16))
    mats = toeplitz(taps_b.astype(jnp.float32))
    blocks = seq // filter_len

    def mask_for(index):
        start = (index * filter_len).astype(jnp.int32)
        target = lax.dynamic_slice_in_dim(all_docs, base + start, filter_len)
        source = lax.dynamic_slice_in_dim(all_docs, margin + start, 2 * filter_len)
        return (target[:, None] == source[None, :]).astype(jnp.float32)

    def forward_block(index):
        start = (index * filter_len).astype(jnp.int32)
        window = lax.dynamic_slice_in_dim(u_window, start, 2 * filter_len, 0).reshape(2 * filter_len, groups, group_width)
        masked = mats * mask_for(index)[None]
        return jnp.einsum('gtj,jgf->tgf', masked, window, precision=lax.Precision.HIGHEST).reshape(filter_len, width)
    conv = lax.map(forward_block, jnp.arange(blocks, dtype=jnp.int32)).reshape(seq, width)
    total = conv + skip_gain[None, :] * u_float
    mixed = (q_feat * total).astype(jnp.bfloat16)
    gradient = cotangent.astype(jnp.float32)
    dq_feat = gradient * total
    dz = gradient * q_feat
    dz_b = lax.optimization_barrier(dz.astype(jnp.bfloat16)).astype(jnp.float32)

    def backward_block(carry, index):
        start = (index * filter_len).astype(jnp.int32)
        window = lax.dynamic_slice_in_dim(u_window, start, 2 * filter_len, 0).reshape(2 * filter_len, groups, group_width)
        target = lax.dynamic_slice_in_dim(dz_b, start, filter_len, 0).reshape(filter_len, groups, group_width)
        mask = mask_for(index)
        contrib = jnp.einsum('gtj,tgf->jgf', mats * mask[None], target, precision=lax.Precision.HIGHEST).reshape(2 * filter_len, width)
        dmat = jnp.einsum('tgf,jgf->gtj', target, window, precision=lax.Precision.HIGHEST) * mask[None]
        return (carry + dmat, contrib)
    dmat_sum, contribs = lax.scan(backward_block, jnp.zeros((groups, filter_len, 2 * filter_len), jnp.float32), jnp.arange(blocks, dtype=jnp.int32))
    lower = contribs[:, :filter_len]
    upper = contribs[:, filter_len:]
    shifted = jnp.concatenate([lower[1:], jnp.zeros((1, filter_len, width), jnp.float32)], 0)
    du_total = (upper + shifted).reshape(seq, width) + skip_gain[None, :] * dz
    unused, pullback = jax.vjp(toeplitz, filter_taps)
    grad_filter = pullback(dmat_sum)[0]
    dk_feat = du_total * v_feat
    dv_feat = du_total * k_feat
    back_docs = all_docs[base:base + seq + margin]
    tail = jnp.zeros((margin, width), jnp.float32)
    grad_query = featurize_back(jnp.concatenate([dq_feat, tail], 0), short_taps[0], back_docs, seq).astype(jnp.bfloat16)
    grad_key = featurize_back(jnp.concatenate([dk_feat, tail], 0), short_taps[1], back_docs, seq).astype(jnp.bfloat16)
    grad_value = featurize_back(jnp.concatenate([dv_feat, tail], 0), short_taps[2], back_docs, seq).astype(jnp.bfloat16)
    grad_short = jnp.stack([tap_grads(dq_feat, q_ext, feat_docs, seq, count_taps), tap_grads(dk_feat, k_ext, feat_docs, seq, count_taps), tap_grads(dv_feat, v_ext, feat_docs, seq, count_taps)])
    grad_skip = lax.optimization_barrier(jnp.sum(dz * u_float, axis=0))
    return (mixed, grad_query, grad_key, grad_value, grad_short, grad_filter, grad_skip)

def reference(query_proj, key_proj, value_proj, short_taps, filter_taps, skip_gain, doc_lengths, out_grad):

    def per_context(items):
        return one_group(items[0], items[1], items[2], items[3], items[4], short_taps, filter_taps, skip_gain)
    results = lax.map(per_context, (query_proj, key_proj, value_proj, out_grad, doc_lengths))
    scale = float(GROUPS * SEQ) ** (-0.5)
    return (results[0], results[1], results[2], results[3], lax.optimization_barrier(jnp.sum(results[4], axis=0)) * scale, lax.optimization_barrier(jnp.sum(results[5], axis=0)) * scale, lax.optimization_barrier(jnp.sum(results[6], axis=0)) * scale)
```

```python
import functools
import math

import jax
import jax.numpy as jnp
from jax import lax
from jax.experimental import pallas as pl
from jax.experimental.pallas import tpu as pltpu
from jax.sharding import PartitionSpec as P

MESH = pl.DeviceIdType.MESH
LANES = 128
HALO = 8
AHEAD = 2


def device(ctx, dp):
    return {"ctx": ctx, "dp": dp}


def block_kernel(
    steps,
    group_width,
    lengths,
    query,
    keys,
    values,
    cotangent,
    taps,
    filters,
    flipped,
    skip,
    mixed,
    grad_query,
    grad_key,
    grad_value,
    partial,
    window,
    feats,
    u_own,
    dz_own,
    u_prior,
    dz_next,
    head_out,
    head_in,
    back_out,
    back_in,
    feat_mask,
    back_mask,
    conv_mask,
    conv_keep,
    du_mask,
    grads,
    tails,
    sums,
    send_u,
    recv_u,
    send_dz,
    recv_dz,
    send_head,
    recv_head,
    send_back,
    recv_back,
):
    me = lax.axis_index("ctx")
    row = lax.axis_index("dp")
    count = lax.axis_size("ctx")
    after, before = lax.rem(me + 1, count), lax.rem(me + count - 1, count)
    tokens = query.shape[0]
    chunk = u_own.shape[2]
    tiles = chunk // LANES
    count_taps = taps.shape[1]
    per_tile = LANES // group_width
    has_prior, has_next = me > 0, me < count - 1
    streams = (query, keys, values)
    outputs = (grad_query, grad_key, grad_value)

    def head_copy(n):
        return pltpu.make_async_remote_copy(
            src_ref=head_out.at[n],
            dst_ref=head_in.at[n],
            send_sem=send_head.at[n],
            recv_sem=recv_head.at[n],
            device_id=device(after, row),
            device_id_type=MESH,
        )

    def u_copy(n):
        return pltpu.make_async_remote_copy(
            src_ref=u_own.at[n],
            dst_ref=u_prior.at[n],
            send_sem=send_u.at[n],
            recv_sem=recv_u.at[n],
            device_id=device(after, row),
            device_id_type=MESH,
        )

    def dz_copy(n):
        return pltpu.make_async_remote_copy(
            src_ref=dz_own.at[n],
            dst_ref=dz_next.at[n],
            send_sem=send_dz.at[n],
            recv_sem=recv_dz.at[n],
            device_id=device(before, row),
            device_id_type=MESH,
        )

    def back_copy(n):
        return pltpu.make_async_remote_copy(
            src_ref=back_out.at[n],
            dst_ref=back_in.at[n],
            send_sem=send_back.at[n],
            recv_sem=recv_back.at[n],
            device_id=device(before, row),
            device_id_type=MESH,
        )

    barrier = pltpu.get_barrier_semaphore()
    for neighbour in (after, before):
        pl.semaphore_signal(
            barrier, inc=1, device_id=device(neighbour, row), device_id_type=MESH
        )

    def stage_head(n, carry):
        lanes = pl.ds(pl.multiple_of(n * chunk, chunk), chunk)
        last = [
            ref[tokens - 16 : tokens, lanes].astype(jnp.float32)[16 - HALO :] for ref in streams
        ]
        blank = jnp.zeros((HALO, chunk), jnp.float32)
        head_out[n] = jnp.concatenate(last + [blank], 0).astype(jnp.bfloat16)
        back_out[n] = jnp.zeros(back_out.shape[1:], jnp.bfloat16)
        return carry

    lax.fori_loop(0, steps, stage_head, 0)

    @pl.when(jnp.logical_not(has_prior))
    def _():
        u_prior[...] = jnp.zeros(u_prior.shape, u_prior.dtype)
        head_in[...] = jnp.zeros(head_in.shape, head_in.dtype)

    @pl.when(jnp.logical_not(has_next))
    def _():
        dz_next[...] = jnp.zeros(dz_next.shape, dz_next.dtype)
        back_in[...] = jnp.zeros(back_in.shape, back_in.dtype)

    pl.semaphore_wait(barrier, 2)

    @pl.when(has_next)
    def _():
        def send_heads(n, carry):
            head_copy(n).start()
            return carry

        lax.fori_loop(0, steps, send_heads, 0)

    starts = [jnp.int32(0)]
    for index in range(lengths.shape[1] - 1):
        starts.append(starts[-1] + lengths[0, index])

    def docs(positions):
        result = jnp.full(positions.shape, -1, jnp.int32)
        for start in starts:
            result = result + (positions >= start).astype(jnp.int32)
        return result

    def iota(shape, dim):
        return lax.broadcasted_iota(jnp.int32, shape, dim)

    anchor = me * tokens
    wide = (tokens, 2 * tokens)
    target, source = iota(wide, 0), iota(wide, 1) - tokens
    lag = target - source
    own_docs = docs(iota((tokens, LANES), 0) + anchor)
    same = jnp.concatenate([own_docs] * (2 * tokens // LANES), 1) == docs(source + anchor)
    conv_mask[...] = jnp.where(same & (lag >= 0) & (lag < tokens), 1.0, 0.0).astype(jnp.bfloat16)
    target = tokens - 1 - target
    lag = target - source
    same = docs(target + anchor) == docs(source + anchor)
    conv_keep[...] = jnp.where(same & (lag >= 0) & (lag < tokens), 1.0, 0.0)
    lag = iota(wide, 1) - iota(wide, 0)
    same = jnp.concatenate([own_docs] * (2 * tokens // LANES), 1) == docs(iota(wide, 1) + anchor)
    du_mask[...] = jnp.where(same & (lag >= 0) & (lag < tokens), 1.0, 0.0).astype(jnp.bfloat16)
    spread = (tokens + HALO, LANES)
    here = iota(spread, 0) - HALO
    here_docs = docs(here + anchor)
    for offset in range(count_taps):
        if offset:
            prior_docs = docs(iota((tokens, LANES), 0) + (anchor - offset))
            feat_mask[offset - 1] = jnp.where(prior_docs == own_docs, 1.0, 0.0)
        there = here + offset
        fits = (there >= 0) & (there < tokens) & (docs(there + anchor) == here_docs)
        back_mask[offset] = jnp.where(fits, 1.0, 0.0)
    for stream in range(3):
        grads[stream, 0:HALO] = jnp.zeros((HALO, LANES), jnp.float32)
        grads[stream, HALO + tokens :] = jnp.zeros((HALO, LANES), jnp.float32)
    sums[...] = jnp.zeros(sums.shape, jnp.float32)
    lane_group = iota((tokens, LANES), 1) // group_width
    opposite = iota((tokens, LANES), 0) + iota((tokens, LANES), 1) == tokens - 1
    upside = jnp.where(opposite, 1.0, 0.0).astype(jnp.bfloat16)

    def featurize(n, i):
        tile = n * tiles + i
        lanes = pl.ds(pl.multiple_of(tile * LANES, LANES), LANES)
        inner = pl.ds(pl.multiple_of(i * LANES, LANES), LANES)
        first = head_in[n, 0:16, inner].astype(jnp.float32)
        second = head_in[n, 16:32, inner].astype(jnp.float32)
        heads = (first[:HALO], first[HALO:], second[:HALO])
        made = []
        for stream in range(3):
            window[tile, stream, 0:HALO] = heads[stream]
            own = streams[stream][:, lanes].astype(jnp.float32)
            window[tile, stream, HALO : HALO + tokens] = own
            result = taps[stream, 0:1, lanes] * own
            for offset in range(1, count_taps):
                shifted = window[tile, stream, HALO - offset : HALO - offset + tokens]
                result = result + taps[stream, offset : offset + 1, lanes] * (
                    shifted * feat_mask[offset - 1]
                )
            feats[tile, stream] = result
            made.append(result)
        u_own[n, :, inner] = (made[1] * made[2]).astype(jnp.bfloat16)
        gradient = cotangent[:, lanes].astype(jnp.float32)
        dz_own[n, :, inner] = (gradient * made[0]).astype(jnp.bfloat16)

    def convolve(n, i):
        tile = n * tiles + i
        lanes = pl.ds(pl.multiple_of(tile * LANES, LANES), LANES)
        inner = pl.ds(pl.multiple_of(i * LANES, LANES), LANES)
        u_tile = u_own[n, :, inner]
        dz_tile = dz_own[n, :, inner]
        dz_turned = jnp.dot(upside, dz_tile, preferred_element_type=jnp.float32)
        dz_turned = dz_turned.astype(jnp.bfloat16)
        u_window = jnp.concatenate([u_prior[n, :, inner], u_tile], 0)
        dz_window = jnp.concatenate([dz_tile, dz_next[n, :, inner]], 0)
        conv = jnp.zeros((tokens, LANES), jnp.float32)
        du = jnp.zeros((tokens, LANES), jnp.float32)
        rows = pl.ds(pl.multiple_of(tile * per_tile, per_tile), per_tile)
        own_taps, own_flipped = filters[rows], flipped[rows]
        for group in range(per_tile):
            mine = lane_group == group

            def circulant(line):
                spread_line = jnp.broadcast_to(line[group : group + 1], (tokens, LANES))
                turned = pltpu.roll(spread_line, 0, 1, stride=1, stride_axis=0)
                half = turned.astype(jnp.bfloat16)
                return jnp.concatenate([half, half], 1)

            piece = jnp.dot(
                circulant(own_flipped) * conv_mask[...],
                u_window,
                preferred_element_type=jnp.float32,
            )
            conv = jnp.where(mine, piece, conv)
            piece = jnp.dot(
                circulant(own_taps) * du_mask[...],
                dz_window,
                preferred_element_type=jnp.float32,
            )
            du = jnp.where(mine, piece, du)
            chosen = jnp.where(mine, dz_turned, jnp.zeros_like(dz_turned))
            outer = lax.dot_general(
                chosen,
                u_window,
                (((1,), (1,)), ((), ())),
                preferred_element_type=jnp.float32,
            )
            outer = outer * conv_keep[...]
            folded = outer[:, :LANES] + outer[:, LANES:]
            turned = pltpu.roll(folded, 0, 1, stride=1, stride_axis=0)
            sums[24 + group : 25 + group] = jnp.sum(turned, axis=0, keepdims=True)
        u_float = u_tile.astype(jnp.float32)
        gradient = cotangent[:, lanes].astype(jnp.float32)
        gain = skip[:, lanes]
        q_feat = feats[tile, 0]
        dz = gradient * q_feat
        total = conv + gain * u_float
        mixed[:, lanes] = (q_feat * total).astype(jnp.bfloat16)
        sums[3 * count_taps : 3 * count_taps + 1] = jnp.sum(dz * u_float, axis=0, keepdims=True)
        du = du + gain * dz
        inside = pl.ds(HALO, tokens)
        grads[0, inside] = gradient * total
        grads[1, inside] = du * feats[tile, 2]
        grads[2, inside] = du * feats[tile, 1]
        heads = []
        for stream in range(3):
            result = None
            x_window = window[tile, stream]
            for offset in range(count_taps):
                shifted = grads[stream, offset : offset + tokens + HALO] * back_mask[offset]
                term = taps[stream, offset : offset + 1, lanes] * shifted
                result = term if result is None else result + term
                line = stream * count_taps + offset
                sums[line : line + 1] = jnp.sum(shifted * x_window, axis=0, keepdims=True)
            heads.append(result[:HALO])
            tails[stream, :, lanes] = result[HALO + tokens - 16 :]
            outputs[stream][:, lanes] = result[HALO:].astype(jnp.bfloat16)
        heads.append(jnp.zeros((HALO, LANES), jnp.float32))
        back_out[n, :, inner] = jnp.concatenate(heads, 0).astype(jnp.bfloat16)
        partial[tile] = sums[...].astype(jnp.bfloat16)

    def step(n, carry):
        @pl.when(n < steps)
        def _():
            @pl.when(has_prior)
            def _():
                head_copy(n).wait_recv()

            def one(i, inside):
                featurize(n, i)
                return inside

            lax.fori_loop(0, tiles, one, 0)

            @pl.when(has_next)
            def _():
                u_copy(n).start()

            @pl.when(has_prior)
            def _():
                dz_copy(n).start()

        @pl.when(n >= AHEAD)
        def _():
            past = n - AHEAD

            @pl.when(has_prior)
            def _():
                u_copy(past).wait_recv()

            @pl.when(has_next)
            def _():
                dz_copy(past).wait_recv()

            def one(i, inside):
                convolve(past, i)
                return inside

            lax.fori_loop(0, tiles, one, 0)

            @pl.when(has_prior)
            def _():
                back_copy(past).start()

        return carry

    lax.fori_loop(0, steps + AHEAD, step, 0)

    def finish(n, carry):
        @pl.when(has_next)
        def _():
            back_copy(n).wait_recv()

        lanes = pl.ds(pl.multiple_of(n * chunk, chunk), chunk)
        first = back_in[n, 0:16].astype(jnp.float32)
        second = back_in[n, 16:32].astype(jnp.float32)
        arrived = (first[:HALO], first[HALO:], second[:HALO])
        for stream in range(3):
            tail = tails[stream, :, lanes]
            fixed = jnp.concatenate([tail[:HALO], tail[HALO:] + arrived[stream]], 0)
            outputs[stream][tokens - 16 : tokens, lanes] = fixed.astype(jnp.bfloat16)

        @pl.when(has_next)
        def _():
            head_copy(n).wait_send()
            u_copy(n).wait_send()

        @pl.when(has_prior)
        def _():
            dz_copy(n).wait_send()
            back_copy(n).wait_send()

        return carry

    lax.fori_loop(0, steps, finish, 0)


def local_block(steps, query, keys, values, cotangent, taps, filters, skip, lengths):
    tokens, width = query.shape
    groups, filter_len = filters.shape
    chunk = width // steps
    tiles = width // LANES
    count_taps = taps.shape[1]
    rounded = filters.astype(jnp.bfloat16).astype(jnp.float32)
    flipped = jnp.concatenate([rounded[:, :1], rounded[:, :0:-1]], 1)
    stream = jax.ShapeDtypeStruct((tokens, width), jnp.bfloat16)
    vmem = pl.BlockSpec(memory_space=pltpu.VMEM)
    dma = pltpu.SemaphoreType.DMA((steps,))
    piece = pltpu.VMEM((steps, tokens, chunk), jnp.bfloat16)
    margin = pltpu.VMEM((steps, 32, chunk), jnp.bfloat16)
    return pl.pallas_call(
        functools.partial(block_kernel, steps, width // groups),
        out_shape=[stream] * 4 + [jax.ShapeDtypeStruct((tiles, 32, LANES), jnp.bfloat16)],
        in_specs=[pl.BlockSpec(memory_space=pltpu.SMEM)] + [vmem] * 8,
        out_specs=[vmem] * 5,
        scratch_shapes=[
            pltpu.VMEM((tiles, 3, tokens + HALO, LANES), jnp.float32),
            pltpu.VMEM((tiles, 3, tokens, LANES), jnp.float32),
            piece,
            piece,
            piece,
            piece,
            margin,
            margin,
            margin,
            margin,
            pltpu.VMEM((count_taps - 1, tokens, LANES), jnp.float32),
            pltpu.VMEM((count_taps, tokens + HALO, LANES), jnp.float32),
            pltpu.VMEM((tokens, 2 * tokens), jnp.bfloat16),
            pltpu.VMEM((tokens, 2 * tokens), jnp.float32),
            pltpu.VMEM((tokens, 2 * tokens), jnp.bfloat16),
            pltpu.VMEM((3, tokens + 2 * HALO, LANES), jnp.float32),
            pltpu.VMEM((3, 16, width), jnp.float32),
            pltpu.VMEM((32, LANES), jnp.float32),
        ]
        + [dma] * 8,
        compiler_params=pltpu.CompilerParams(
            collective_id=0, has_side_effects=True, vmem_limit_bytes=56 * 2**20
        ),
        name="block",
    )(lengths, query, keys, values, cotangent, taps, rounded, flipped, skip)


def reduce_kernel(
    scale,
    partial,
    result,
    gathered,
    stacked,
    spread_sums,
    send_one,
    recv_one,
    send_two,
    recv_two,
    send_three,
    recv_three,
):
    ctx, dp = lax.axis_index("ctx"), lax.axis_index("dp")
    x, high, core = ctx // 4, lax.rem(ctx // 2, 2), lax.rem(ctx, 2)
    low, y = dp // 4, lax.rem(dp, 4)
    place = (x * 2 + core) * 4 + y
    depth = high * 4 + low
    planes = gathered.shape[0]
    depths = stacked.shape[0]

    def in_plane(index):
        return device(
            (index // 8) * 4 + high * 2 + lax.rem(index // 4, 2), low * 4 + lax.rem(index, 4)
        )

    def in_depth(index):
        return device(x * 4 + (index // 4) * 2 + core, lax.rem(index, 4) * 4 + y)

    def first(peer, slot):
        return pltpu.make_async_remote_copy(
            src_ref=partial.at[peer],
            dst_ref=gathered.at[slot],
            send_sem=send_one.at[peer],
            recv_sem=recv_one.at[slot],
            device_id=in_plane(peer),
            device_id_type=MESH,
        )

    def second(peer, slot):
        return pltpu.make_async_remote_copy(
            src_ref=stacked.at[depth],
            dst_ref=stacked.at[slot],
            send_sem=send_two.at[peer],
            recv_sem=recv_two.at[slot],
            device_id=in_depth(peer),
            device_id_type=MESH,
        )

    def third(peer, slot):
        return pltpu.make_async_remote_copy(
            src_ref=spread_sums.at[place],
            dst_ref=spread_sums.at[slot],
            send_sem=send_three.at[peer],
            recv_sem=recv_three.at[slot],
            device_id=in_plane(peer),
            device_id_type=MESH,
        )

    def each(count, mine, action):
        def body(k, carry):
            action(lax.rem(mine + k, count))
            return carry

        lax.fori_loop(1, count, body, 0)

    barrier = pltpu.get_barrier_semaphore()

    def greet(where):
        def action(peer):
            pl.semaphore_signal(barrier, inc=1, device_id=where(peer), device_id_type=MESH)

        return action

    each(planes, place, greet(in_plane))
    each(depths, depth, greet(in_depth))
    pl.semaphore_wait(barrier, planes + depths - 2)

    each(planes, place, lambda peer: first(peer, place).start())
    gathered[place] = partial[place]
    each(planes, place, lambda peer: first(peer, peer).wait_recv())
    total = gathered[0].astype(jnp.float32)
    for index in range(1, planes):
        total = total + gathered[index].astype(jnp.float32)
    stacked[depth] = total
    each(depths, depth, lambda peer: second(peer, depth).start())
    each(depths, depth, lambda peer: second(peer, peer).wait_recv())
    total = stacked[0]
    for index in range(1, depths):
        total = total + stacked[index]
    spread_sums[place] = (total * scale).astype(jnp.bfloat16)
    each(planes, place, lambda peer: third(peer, place).start())
    each(planes, place, lambda peer: third(peer, peer).wait_recv())
    result[...] = spread_sums[...]
    each(planes, place, lambda peer: first(peer, place).wait_send())
    each(depths, depth, lambda peer: second(peer, depth).wait_send())
    each(planes, place, lambda peer: third(peer, place).wait_send())


def reduced(partial, scale):
    planes, rows, lanes = partial.shape
    depths = 8
    vmem = pl.BlockSpec(memory_space=pltpu.VMEM)
    plane_sems = pltpu.SemaphoreType.DMA((planes,))
    depth_sems = pltpu.SemaphoreType.DMA((depths,))
    return pl.pallas_call(
        functools.partial(reduce_kernel, scale),
        out_shape=jax.ShapeDtypeStruct(partial.shape, jnp.bfloat16),
        in_specs=[vmem],
        out_specs=vmem,
        scratch_shapes=[
            pltpu.VMEM((planes, rows, lanes), jnp.bfloat16),
            pltpu.VMEM((depths, rows, lanes), jnp.float32),
            pltpu.VMEM((planes, rows, lanes), jnp.bfloat16),
            plane_sems,
            plane_sems,
            depth_sems,
            depth_sems,
            plane_sems,
            plane_sems,
        ],
        compiler_params=pltpu.CompilerParams(
            collective_id=1, has_side_effects=True, vmem_limit_bytes=16 * 2**20
        ),
        name="reduce",
    )(partial)


def shards(
    query_proj, key_proj, value_proj, short_taps, filter_taps, skip_gain, doc_lengths, out_grad
):
    tokens, width = query_proj.shape[1:]
    count_taps = short_taps.shape[1]
    mixed, grad_query, grad_key, grad_value, partial = local_block(
        8,
        query_proj[0],
        key_proj[0],
        value_proj[0],
        out_grad[0],
        short_taps,
        filter_taps,
        skip_gain[None],
        doc_lengths,
    )
    scale = 1.0 / math.sqrt(tokens * lax.axis_size("ctx") * lax.axis_size("dp"))
    sums = reduced(partial, scale).astype(jnp.float32)
    lines = 3 * count_taps
    short = sums[:, :lines].transpose(1, 0, 2).reshape(3, count_taps, width)
    gain = sums[:, lines].reshape(width)
    folded = sums[:, 24:].reshape(filter_taps.shape)
    filters = folded[:, ::-1]
    return (
        mixed[None],
        grad_query[None],
        grad_key[None],
        grad_value[None],
        short,
        filters,
        gain,
    )


def solution(mesh):
    return jax.shard_map(
        shards,
        mesh=mesh,
        in_specs=(
            P("dp", "ctx", None),
            P("dp", "ctx", None),
            P("dp", "ctx", None),
            P(),
            P(),
            P(),
            P("dp", None),
            P("dp", "ctx", None),
        ),
        out_specs=(
            P("dp", "ctx", None),
            P("dp", "ctx", None),
            P("dp", "ctx", None),
            P("dp", "ctx", None),
            P(),
            P(),
            P(),
        ),
        check_vma=False,
    )
```

```python
import functools
import math

import jax
import jax.numpy as jnp
from jax import lax
from jax.experimental import pallas as pl
from jax.experimental.pallas import tpu as pltpu
from jax.sharding import PartitionSpec as P

MESH = pl.DeviceIdType.MESH
LANES = 128
HALO = 8
STEPS = 8
AHEAD = 3
LEAD = 2
EARLY = 2
EDGE = 16
REFINE = 1


def device(ctx, dp):
    return {"ctx": ctx, "dp": dp}


def block_kernel(
    steps,
    group_width,
    scale,
    lengths,
    query,
    keys,
    values,
    cotangent,
    taps,
    filters,
    skip,
    mixed,
    grad_query,
    grad_key,
    grad_value,
    spread_sums,
    inputs,
    results,
    tails,
    window,
    feats,
    flipped,
    u_own,
    dz_own,
    u_prior,
    dz_next,
    head_out,
    head_in,
    back_out,
    back_in,
    heads,
    packed,
    places,
    feat_mask,
    back_mask,
    conv_mask,
    conv_keep,
    du_mask,
    grads,
    sums,
    partial,
    gathered,
    stacked,
    load_sem,
    store_sem,
    tail_sem,
    send_u,
    recv_u,
    send_dz,
    recv_dz,
    send_head,
    recv_head,
    send_back,
    recv_back,
    send_one,
    recv_one,
    send_two,
    recv_two,
    send_three,
    recv_three,
):
    me = lax.axis_index("ctx")
    row = lax.axis_index("dp")
    count = lax.axis_size("ctx")
    after, before = lax.rem(me + 1, count), lax.rem(me + count - 1, count)
    tokens, width = query.shape
    chunk = width // steps
    tiles = chunk // LANES
    count_taps = taps.shape[1]
    margin = count_taps - 1
    per_tile = LANES // group_width
    has_prior, has_next = me > 0, me < count - 1
    sources = (query, keys, values, cotangent)
    outputs = (mixed, grad_query, grad_key, grad_value)

    x, high, core = me // 4, lax.rem(me // 2, 2), lax.rem(me, 2)
    low, y = row // 4, lax.rem(row, 4)
    place = (x * 2 + core) * 4 + y
    depth = high * 4 + low
    planes = gathered.shape[0]
    depths = stacked.shape[0]
    owned = place // tiles

    def in_plane(index):
        return device(
            (index // 8) * 4 + high * 2 + lax.rem(index // 4, 2), low * 4 + lax.rem(index, 4)
        )

    def in_depth(index):
        return device(x * 4 + (index // 4) * 2 + core, lax.rem(index, 4) * 4 + y)

    def remote(source, target, send, recv, where):
        return pltpu.make_async_remote_copy(
            src_ref=source,
            dst_ref=target,
            send_sem=send,
            recv_sem=recv,
            device_id=where,
            device_id_type=MESH,
        )

    def head_copy(n):
        return remote(
            head_out.at[n], head_in.at[n], send_head.at[n], recv_head.at[n], device(after, row)
        )

    parts = (pl.ds(EDGE, tokens - EDGE), pl.ds(0, EDGE))

    def u_copy(n, part):
        rows = parts[part]
        return remote(
            u_own.at[n, rows], u_prior.at[n, rows], send_u.at[n, part], recv_u.at[n, part],
            device(after, row),
        )

    def dz_copy(n, part):
        rows = parts[part]
        return remote(
            dz_own.at[n, rows], dz_next.at[n, rows], send_dz.at[n, part], recv_dz.at[n, part],
            device(before, row),
        )

    def send_part(n, part):
        @pl.when(has_next)
        def _():
            u_copy(n, part).start()

        @pl.when(has_prior)
        def _():
            dz_copy(n, part).start()

    def back_copy(n):
        return remote(
            back_out.at[n], back_in.at[n], send_back.at[n], recv_back.at[n], device(before, row)
        )

    def first(peer, slot):
        return remote(
            partial.at[peer], gathered.at[slot], send_one.at[peer], recv_one.at[slot],
            in_plane(peer),
        )

    def second(peer, slot):
        return remote(
            stacked.at[depth], stacked.at[slot], send_two.at[peer], recv_two.at[slot],
            in_depth(peer),
        )

    def third(peer, slot):
        return remote(
            spread_sums.at[place], spread_sums.at[slot], send_three.at[peer],
            recv_three.at[slot], in_plane(peer),
        )

    def load(n, which):
        lanes = pl.ds(pl.multiple_of(n * chunk, chunk), chunk)
        return pltpu.make_async_copy(
            sources[which].at[:, lanes], inputs.at[n, which], load_sem.at[n, which]
        )

    def save(n, which):
        lanes = pl.ds(pl.multiple_of(n * chunk, chunk), chunk)
        rows = pl.ds(0, tokens if which == 0 else tokens - 16)
        return pltpu.make_async_copy(
            results.at[n, which, rows], outputs[which].at[rows, lanes], store_sem.at[n, which]
        )

    def save_tail(n, stream):
        lanes = pl.ds(pl.multiple_of(n * chunk, chunk), chunk)
        rows = pl.ds(tokens - 16, 16)
        return pltpu.make_async_copy(
            results.at[n, 1 + stream, rows],
            outputs[1 + stream].at[rows, lanes],
            tail_sem.at[n, stream],
        )

    def each(size, mine, action):
        for k in range(1, size):
            action(lax.rem(mine + k, size))

    def over(size, action):
        def body(k, carry):
            action(k)
            return carry

        lax.fori_loop(0, size, body, 0)

    def load_all(n):
        for which in (1, 2, 0, 3):
            load(n, which).start()

    over(steps, load_all)

    barrier = pltpu.get_barrier_semaphore()

    def greet(where):
        pl.semaphore_signal(barrier, inc=1, device_id=where, device_id_type=MESH)

    greet(device(after, row))
    greet(device(before, row))
    for k in range(1, planes):
        greet(in_plane(lax.rem(place + k, planes)))
    for k in range(1, depths):
        greet(in_depth(lax.rem(depth + k, depths)))

    starts = [jnp.int32(0)]
    for index in range(lengths.shape[1] - 1):
        starts.append(starts[-1] + lengths[0, index])

    def docs(positions):
        result = jnp.full(positions.shape, -1, jnp.int32)
        for start in starts:
            result = result + (positions >= start).astype(jnp.int32)
        return result

    def iota(shape, dim):
        return lax.broadcasted_iota(jnp.int32, shape, dim)

    anchor = me * tokens
    reach = tokens + 2 * HALO
    places[...] = docs(iota((reach, LANES), 0) + (anchor - HALO))
    own_docs = places[HALO : HALO + tokens]
    for offset in range(1, count_taps):
        prior_docs = places[HALO - offset : HALO - offset + tokens]
        feat_mask[offset - 1] = jnp.where(prior_docs == own_docs, 1.0, 0.0)
    spread = tokens + HALO
    here = iota((spread, LANES), 0) - HALO
    here_docs = places[0:spread]
    for offset in range(count_taps):
        there = here + offset
        fits = (there >= 0) & (there < tokens) & (places[offset : offset + spread] == here_docs)
        back_mask[offset] = jnp.where(fits, 1.0, 0.0)
    wide = (tokens, 2 * tokens)
    across = docs(iota((8, 3 * tokens), 1) + (anchor - tokens))[0:1]
    source_docs = jnp.broadcast_to(across[:, : 2 * tokens], wide)
    target_docs = jnp.broadcast_to(across[:, tokens:], wide)
    down = iota(wide, 0)
    side = iota(wide, 1)
    twice = jnp.concatenate([own_docs, own_docs], 1)
    lag = down - side + tokens
    fits = (twice == source_docs) & (lag >= 0) & (lag < tokens)
    conv_mask[...] = jnp.where(fits, 1.0, 0.0).astype(jnp.bfloat16)
    lag = side - down
    fits = (twice == target_docs) & (lag >= 0) & (lag < tokens)
    du_mask[...] = jnp.where(fits, 1.0, 0.0).astype(jnp.bfloat16)
    turned_docs = docs((anchor + tokens - 1) - iota((tokens, LANES), 0))
    twice = jnp.concatenate([turned_docs, turned_docs], 1)
    lag = 2 * tokens - 1 - down - side
    fits = (twice == source_docs) & (lag >= 0) & (lag < tokens)
    conv_keep[...] = jnp.where(fits, 1.0, 0.0)
    for stream in range(3):
        grads[stream, 0:HALO] = jnp.zeros((HALO, LANES), jnp.float32)
        grads[stream, HALO + tokens :] = jnp.zeros((HALO, LANES), jnp.float32)
    sums[...] = jnp.zeros(sums.shape, jnp.float32)
    packed[...] = jnp.zeros(packed.shape, jnp.float32)

    def clear(tile):
        for stream in range(3):
            window[tile, stream, 0:HALO] = jnp.zeros((HALO, LANES), jnp.float32)

    over(width // LANES, clear)
    lane_group = iota((tokens, LANES), 1) // group_width
    square = (LANES, LANES)
    turn = (iota(square, 0) + iota(square, 1)) % LANES == 0
    flipped[...] = jnp.dot(
        filters[...].astype(jnp.bfloat16),
        jnp.where(turn, 1.0, 0.0).astype(jnp.bfloat16),
        preferred_element_type=jnp.float32,
    )
    opposite = iota((tokens, LANES), 0) + iota((tokens, LANES), 1) == tokens - 1
    upside = jnp.where(opposite, 1.0, 0.0).astype(jnp.bfloat16)

    @pl.when(jnp.logical_not(has_prior))
    def _():
        u_prior[...] = jnp.zeros(u_prior.shape, u_prior.dtype)
        head_in[...] = jnp.zeros(head_in.shape, head_in.dtype)

    @pl.when(jnp.logical_not(has_next))
    def _():
        dz_next[...] = jnp.zeros(dz_next.shape, dz_next.dtype)
        back_in[...] = jnp.zeros(back_in.shape, back_in.dtype)

    def spot(i, stream):
        at = (i * 3 + stream) * margin
        return slice(at, at + margin)

    def stage_head(n):
        for which in (1, 2, 0):
            load(n, which).wait()
        for i in range(tiles):
            for stream in range(3):
                last = inputs[n, stream, tokens - 16 : tokens, i * LANES : (i + 1) * LANES]
                packed[spot(i, stream)] = last.astype(jnp.float32)[16 - margin :]
        head_out[n] = packed[...].astype(jnp.bfloat16)

    def send_head_on(n):
        @pl.when(has_next)
        def _():
            head_copy(n).start()

    def open_heads(n):
        packed[...] = head_in[n].astype(jnp.float32)
        for i in range(tiles):
            for stream in range(3):
                window[n * tiles + i, stream, HALO - margin : HALO] = packed[spot(i, stream)]

    def featurize(n, i):
        tile = n * tiles + i
        lanes = pl.ds(pl.multiple_of(tile * LANES, LANES), LANES)
        inner = pl.ds(pl.multiple_of(i * LANES, LANES), LANES)
        made = []
        for stream in range(3):
            own = inputs[n, stream, :, inner].astype(jnp.float32)
            window[tile, stream, HALO : HALO + tokens] = own
            own = own[EDGE:]
            result = taps[stream, 0:1, lanes] * own
            for offset in range(1, count_taps):
                start = HALO + EDGE - offset
                shifted = window[tile, stream, start : start + tokens - EDGE]
                result = result + taps[stream, offset : offset + 1, lanes] * (
                    shifted * feat_mask[offset - 1, EDGE:]
                )
            feats[tile, stream, EDGE:] = result
            made.append(result)
        u_own[n, EDGE:, inner] = (made[1] * made[2]).astype(jnp.bfloat16)
        gradient = inputs[n, 3, EDGE:, inner].astype(jnp.float32)
        dz_own[n, EDGE:, inner] = (gradient * made[0]).astype(jnp.bfloat16)

    def refine(n, i):
        tile = n * tiles + i
        lanes = pl.ds(pl.multiple_of(tile * LANES, LANES), LANES)
        inner = pl.ds(pl.multiple_of(i * LANES, LANES), LANES)
        made = []
        for stream in range(3):
            result = taps[stream, 0:1, lanes] * window[tile, stream, HALO : HALO + EDGE]
            for offset in range(1, count_taps):
                start = HALO - offset
                shifted = window[tile, stream, start : start + EDGE]
                result = result + taps[stream, offset : offset + 1, lanes] * (
                    shifted * feat_mask[offset - 1, 0:EDGE]
                )
            feats[tile, stream, 0:EDGE] = result
            made.append(result)
        u_own[n, 0:EDGE, inner] = (made[1] * made[2]).astype(jnp.bfloat16)
        gradient = inputs[n, 3, 0:EDGE, inner].astype(jnp.float32)
        dz_own[n, 0:EDGE, inner] = (gradient * made[0]).astype(jnp.bfloat16)

    def convolve(n, i):
        tile = n * tiles + i
        lanes = pl.ds(pl.multiple_of(tile * LANES, LANES), LANES)
        inner = pl.ds(pl.multiple_of(i * LANES, LANES), LANES)
        u_tile = u_own[n, :, inner]
        dz_tile = dz_own[n, :, inner]
        dz_turned = jnp.dot(upside, dz_tile, preferred_element_type=jnp.float32)
        dz_turned = dz_turned.astype(jnp.bfloat16)
        u_window = jnp.concatenate([u_prior[n, :, inner], u_tile], 0)
        dz_window = jnp.concatenate([dz_tile, dz_next[n, :, inner]], 0)
        conv = jnp.zeros((tokens, LANES), jnp.float32)
        du = jnp.zeros((tokens, LANES), jnp.float32)
        rows = pl.ds(pl.multiple_of(tile * per_tile, per_tile), per_tile)
        own_taps, own_flipped = filters[rows], flipped[rows]
        for group in range(per_tile):
            mine = lane_group == group

            def circulant(line):
                spread_line = jnp.broadcast_to(line[group : group + 1], (tokens, LANES))
                turned = pltpu.roll(spread_line, 0, 1, stride=1, stride_axis=0)
                half = turned.astype(jnp.bfloat16)
                return jnp.concatenate([half, half], 1)

            piece = jnp.dot(
                circulant(own_flipped) * conv_mask[...],
                u_window,
                preferred_element_type=jnp.float32,
            )
            conv = jnp.where(mine, piece, conv)
            piece = jnp.dot(
                circulant(own_taps) * du_mask[...],
                dz_window,
                preferred_element_type=jnp.float32,
            )
            du = jnp.where(mine, piece, du)
            chosen = jnp.where(mine, dz_turned, jnp.zeros_like(dz_turned))
            outer = lax.dot_general(
                chosen,
                u_window,
                (((1,), (1,)), ((), ())),
                preferred_element_type=jnp.float32,
            )
            outer = outer * conv_keep[...]
            folded = outer[:, :LANES] + outer[:, LANES:]
            turned = pltpu.roll(folded, 0, 1, stride=1, stride_axis=0)
            sums[24 + group : 25 + group] = jnp.sum(turned, axis=0, keepdims=True)
        u_float = u_tile.astype(jnp.float32)
        gradient = inputs[n, 3, :, inner].astype(jnp.float32)
        gain = skip[:, lanes]
        q_feat = feats[tile, 0]
        dz = gradient * q_feat
        total = conv + gain * u_float
        results[n, 0, :, inner] = (q_feat * total).astype(jnp.bfloat16)
        sums[count_taps : count_taps + 1] = jnp.sum(dz * u_float, axis=0, keepdims=True)
        du = du + gain * dz
        inside = pl.ds(HALO, tokens)
        grads[0, inside] = gradient * total
        grads[1, inside] = du * feats[tile, 2]
        grads[2, inside] = du * feats[tile, 1]
        for stream in range(3):
            result = None
            x_window = window[tile, stream]
            for offset in range(count_taps):
                shifted = grads[stream, offset : offset + tokens + HALO] * back_mask[offset]
                term = taps[stream, offset : offset + 1, lanes] * shifted
                result = term if result is None else result + term
                line = stream * 8 + offset
                sums[line : line + 1] = jnp.sum(shifted * x_window, axis=0, keepdims=True)
            heads[i, stream] = result[:HALO]
            tails[stream, :, lanes] = result[HALO + tokens - 16 :]
            whole = result[HALO : HALO + tokens - 16]
            results[n, 1 + stream, 0 : tokens - 16, inner] = whole.astype(jnp.bfloat16)
        partial[tile] = sums[...].astype(jnp.bfloat16)

        @pl.when(tile != place)
        def _():
            first(tile, place).start()

    def gather_own():
        gathered[place] = partial[place]
        each(planes, place, lambda peer: first(peer, peer).wait_recv())
        total = gathered[0].astype(jnp.float32)
        for index in range(1, planes):
            total = total + gathered[index].astype(jnp.float32)
        stacked[depth] = total.astype(jnp.bfloat16)
        each(depths, depth, lambda peer: second(peer, depth).start())

    def spread_own():
        each(depths, depth, lambda peer: second(peer, peer).wait_recv())
        total = stacked[0].astype(jnp.float32)
        for index in range(1, depths):
            total = total + stacked[index].astype(jnp.float32)
        spread_sums[place] = (total * scale).astype(jnp.bfloat16)
        each(planes, place, lambda peer: third(peer, place).start())

    def prepare(n):
        load(n, 3).wait()
        over(tiles, lambda i: featurize(n, i))

    over(LEAD, stage_head)
    over(EARLY, prepare)
    pl.semaphore_wait(barrier, planes + depths)
    over(LEAD, send_head_on)

    def step(n):
        @pl.when(n + LEAD < steps)
        def _():
            stage_head(n + LEAD)
            send_head_on(n + LEAD)

        @pl.when(n < steps)
        def _():
            @pl.when(n >= EARLY)
            def _():
                prepare(n)

            send_part(n, 0)

        ready = n - REFINE

        @pl.when((ready >= 0) & (ready < steps))
        def _():
            @pl.when(has_prior)
            def _():
                head_copy(ready).wait_recv()

            open_heads(ready)
            over(tiles, lambda i: refine(ready, i))
            send_part(ready, 1)

        past = n - AHEAD

        @pl.when(past >= 0)
        def _():
            @pl.when(has_prior)
            def _():
                u_copy(past, 0).wait_recv()
                u_copy(past, 1).wait_recv()

            @pl.when(has_next)
            def _():
                dz_copy(past, 0).wait_recv()
                dz_copy(past, 1).wait_recv()

            over(tiles, lambda i: convolve(past, i))
            packed[...] = jnp.zeros(packed.shape, jnp.float32)
            for i in range(tiles):
                for stream in range(3):
                    packed[spot(i, stream)] = heads[i, stream, HALO - margin : HALO]
            back_out[past] = packed[...].astype(jnp.bfloat16)

            for which in range(4):
                save(past, which).start()

            @pl.when(past == owned + 1)
            def _():
                gather_own()

            @pl.when(past == owned + 2)
            def _():
                spread_own()

    over(steps + AHEAD, step)

    @pl.when(owned == steps - 1)
    def _():
        gather_own()

    @pl.when(has_prior)
    def _():
        over(steps, lambda n: back_copy(n).start())

    @pl.when(owned >= steps - 2)
    def _():
        spread_own()

    def settle(n):
        @pl.when(has_next)
        def _():
            back_copy(n).wait_recv()

        packed[...] = back_in[n].astype(jnp.float32)
        for i in range(tiles):
            lanes = pl.ds(pl.multiple_of(n * chunk + i * LANES, LANES), LANES)
            for stream in range(3):
                tails[stream, 16 - margin : 16, lanes] += packed[spot(i, stream)]
                fixed = tails[stream, :, lanes].astype(jnp.bfloat16)
                results[n, 1 + stream, tokens - 16 : tokens, i * LANES : (i + 1) * LANES] = fixed
        for stream in range(3):
            save_tail(n, stream).start()

    def drain(n):
        for which in range(4):
            save(n, which).wait()
        for stream in range(3):
            save_tail(n, stream).wait()

        @pl.when(has_next)
        def _():
            head_copy(n).wait_send()
            u_copy(n, 0).wait_send()
            u_copy(n, 1).wait_send()

        @pl.when(has_prior)
        def _():
            dz_copy(n, 0).wait_send()
            dz_copy(n, 1).wait_send()
            back_copy(n).wait_send()

    over(steps, settle)
    over(steps, drain)
    each(planes, place, lambda peer: first(peer, place).wait_send())
    each(depths, depth, lambda peer: second(peer, depth).wait_send())
    each(planes, place, lambda peer: third(peer, peer).wait_recv())
    each(planes, place, lambda peer: third(peer, place).wait_send())


def finish_kernel(
    mixed_in,
    query_in,
    key_in,
    value_in,
    sums_in,
    mixed,
    grad_query,
    grad_key,
    grad_value,
    short_out,
    filters_out,
    skip_out,
    sums,
    short,
    filters,
    skip,
    opened,
    stage,
    loaded,
    copied,
    other,
):
    pairs = (mixed_in, mixed), (query_in, grad_query), (key_in, grad_key), (value_in, grad_value)
    parts = copied.shape[1]
    half = mixed.shape[0] // parts
    loads, saves = [], []
    for index, (given, out) in enumerate(pairs):
        for part in range(parts):
            rows = pl.ds(part * half, half)
            here = stage.at[index, rows]
            loads.append(pltpu.make_async_copy(given.at[rows], here, loaded.at[index, part]))
            saves.append(pltpu.make_async_copy(here, out.at[rows], copied.at[index, part]))
    first = pltpu.make_async_copy(sums_in, sums, other.at[0])
    first.start()
    for copy in loads:
        copy.start()
    tiles = sums.shape[0]
    count_taps = short.shape[1]
    per_tile = filters.shape[0] // tiles
    square = (LANES, LANES)
    turn = lax.broadcasted_iota(jnp.int32, square, 0) + lax.broadcasted_iota(jnp.int32, square, 1)
    turn = jnp.where(turn == LANES - 1, 1.0, 0.0).astype(jnp.bfloat16)

    first.wait()
    for i in range(tiles):
        lanes = slice(i * LANES, (i + 1) * LANES)
        opened[i] = sums[i].astype(jnp.float32)
        for stream in range(3):
            short[stream, :, lanes] = opened[i, stream * 8 : stream * 8 + count_taps]
        skip[:, lanes] = opened[i, count_taps : count_taps + 1]
        filters[i * per_tile : (i + 1) * per_tile] = jnp.dot(
            opened[i, 24:].astype(jnp.bfloat16), turn, preferred_element_type=jnp.float32
        )
    pieces = ((short, short_out), (filters, filters_out), (skip, skip_out))
    for index, (given, out) in enumerate(pieces):
        saves.append(pltpu.make_async_copy(given, out, other.at[1 + index]))
        saves[-1].start()
    for coming, leaving in zip(loads, saves):
        coming.wait()
        leaving.start()
    for copy in saves:
        copy.wait()


def local_block(scale, query, keys, values, cotangent, taps, filters, skip, lengths):
    steps = STEPS
    tokens, width = query.shape
    groups = filters.shape[0]
    chunk = width // steps
    tiles = width // LANES
    count_taps = taps.shape[1]
    spots = -(-3 * (count_taps - 1) * (chunk // LANES) // 16) * 16
    bf16, f32 = jnp.bfloat16, jnp.float32
    stream = jax.ShapeDtypeStruct((tokens, width), bf16)
    vmem = pl.BlockSpec(memory_space=pltpu.VMEM)
    hbm = pl.BlockSpec(memory_space=pl.ANY)
    dma = pltpu.SemaphoreType.DMA((steps,))
    pair = pltpu.SemaphoreType.DMA((steps, 2))
    plane = pltpu.SemaphoreType.DMA((32,))
    depth = pltpu.SemaphoreType.DMA((8,))
    piece = pltpu.VMEM((steps, tokens, chunk), bf16)
    margin = pltpu.VMEM((steps, spots, LANES), bf16)
    made = pl.pallas_call(
        functools.partial(block_kernel, steps, width // groups, scale),
        out_shape=[stream] * 4
        + [jax.ShapeDtypeStruct((tiles, 32, LANES), bf16)],
        in_specs=[pl.BlockSpec(memory_space=pltpu.SMEM)] + [hbm] * 4 + [vmem] * 3,
        out_specs=[hbm] * 4 + [vmem],
        scratch_shapes=[
            pltpu.VMEM((steps, 4, tokens, chunk), bf16),
            pltpu.VMEM((steps, 4, tokens, chunk), bf16),
            pltpu.VMEM((3, 16, width), f32),
            pltpu.VMEM((tiles, 3, tokens + HALO, LANES), f32),
            pltpu.VMEM((tiles, 3, tokens, LANES), f32),
            pltpu.VMEM((groups, LANES), f32),
            piece,
            piece,
            piece,
            piece,
            margin,
            margin,
            margin,
            margin,
            pltpu.VMEM((chunk // LANES, 3, HALO, LANES), f32),
            pltpu.VMEM((spots, LANES), f32),
            pltpu.VMEM((tokens + 2 * HALO, LANES), jnp.int32),
            pltpu.VMEM((count_taps - 1, tokens, LANES), f32),
            pltpu.VMEM((count_taps, tokens + HALO, LANES), f32),
            pltpu.VMEM((tokens, 2 * tokens), bf16),
            pltpu.VMEM((tokens, 2 * tokens), f32),
            pltpu.VMEM((tokens, 2 * tokens), bf16),
            pltpu.VMEM((3, tokens + 2 * HALO, LANES), f32),
            pltpu.VMEM((32, LANES), f32),
            pltpu.VMEM((tiles, 32, LANES), bf16),
            pltpu.VMEM((32, 32, LANES), bf16),
            pltpu.VMEM((8, 32, LANES), bf16),
            pltpu.SemaphoreType.DMA((steps, 4)),
            pltpu.SemaphoreType.DMA((steps, 4)),
            pltpu.SemaphoreType.DMA((steps, 3)),
        ]
        + [pair] * 4
        + [dma] * 4
        + [plane, plane, depth, depth, plane, plane],
        compiler_params=pltpu.CompilerParams(
            collective_id=0, has_side_effects=True, vmem_limit_bytes=56 * 2**20
        ),
        name="block",
    )(lengths, query, keys, values, cotangent, taps, filters, skip)
    return pl.pallas_call(
        finish_kernel,
        out_shape=[stream] * 4
        + [
            jax.ShapeDtypeStruct(taps.shape, f32),
            jax.ShapeDtypeStruct(filters.shape, f32),
            jax.ShapeDtypeStruct(skip.shape, f32),
        ],
        in_specs=[hbm] * 5,
        out_specs=[hbm] * 7,
        scratch_shapes=[
            pltpu.VMEM((tiles, 32, LANES), bf16),
            pltpu.VMEM(taps.shape, f32),
            pltpu.VMEM(filters.shape, f32),
            pltpu.VMEM(skip.shape, f32),
            pltpu.VMEM((tiles, 32, LANES), f32),
            pltpu.VMEM((4, tokens, width), bf16),
            pltpu.SemaphoreType.DMA((4, 4)),
            pltpu.SemaphoreType.DMA((4, 4)),
            pltpu.SemaphoreType.DMA((4,)),
        ],
        compiler_params=pltpu.CompilerParams(vmem_limit_bytes=60 * 2**20),
        name="finish",
    )(*made)


def shards(
    query_proj, key_proj, value_proj, short_taps, filter_taps, skip_gain, doc_lengths, out_grad
):
    tokens = query_proj.shape[1]
    scale = 1.0 / math.sqrt(tokens * lax.axis_size("ctx") * lax.axis_size("dp"))
    mixed, grad_query, grad_key, grad_value, short, filters, gain = local_block(
        scale,
        query_proj[0],
        key_proj[0],
        value_proj[0],
        out_grad[0],
        short_taps,
        filter_taps,
        skip_gain[None],
        doc_lengths,
    )
    return (
        mixed[None],
        grad_query[None],
        grad_key[None],
        grad_value[None],
        short,
        filters,
        gain[0],
    )


def solution(mesh):
    return jax.shard_map(
        shards,
        mesh=mesh,
        in_specs=(
            P("dp", "ctx", None),
            P("dp", "ctx", None),
            P("dp", "ctx", None),
            P(),
            P(),
            P(),
            P("dp", None),
            P("dp", "ctx", None),
        ),
        out_specs=(
            P("dp", "ctx", None),
            P("dp", "ctx", None),
            P("dp", "ctx", None),
            P("dp", "ctx", None),
            P(),
            P(),
            P(),
        ),
        check_vma=False,
    )
```

```python
import functools
import math

import jax
import jax.numpy as jnp
from jax import lax
from jax.experimental import pallas as pl
from jax.experimental.pallas import tpu as pltpu
from jax.sharding import PartitionSpec as P

MESH = pl.DeviceIdType.MESH
LANES = 128
HALO = 8
STEPS = 8
OUTER, INNER = 3, 4
LEAD = 2
EARLY = 2
EDGE = 16
REFINE = 1


def device(ctx, dp):
    return {"ctx": ctx, "dp": dp}


def block_kernel(
    steps,
    group_width,
    scale,
    lengths,
    query,
    keys,
    values,
    cotangent,
    taps,
    filters,
    skip,
    mixed,
    grad_query,
    grad_key,
    grad_value,
    spread_sums,
    inputs,
    results,
    tails,
    window,
    feats,
    flipped,
    u_own,
    dz_own,
    u_prior,
    dz_next,
    head_out,
    head_in,
    back_out,
    back_in,
    heads,
    packed,
    places,
    feat_mask,
    back_mask,
    conv_mask,
    conv_keep,
    du_mask,
    grads,
    sums,
    partial,
    gathered,
    stacked,
    load_sem,
    store_sem,
    tail_sem,
    send_u,
    recv_u,
    send_dz,
    recv_dz,
    send_head,
    recv_head,
    send_back,
    recv_back,
    send_one,
    recv_one,
    send_two,
    recv_two,
    send_three,
    recv_three,
):
    me = lax.axis_index("ctx")
    row = lax.axis_index("dp")
    count = lax.axis_size("ctx")
    after, before = lax.rem(me + 1, count), lax.rem(me + count - 1, count)
    tokens, width = query.shape
    chunk = width // steps
    tiles = chunk // LANES
    count_taps = taps.shape[1]
    margin = count_taps - 1
    per_tile = LANES // group_width
    has_prior, has_next = me > 0, me < count - 1
    sources = (query, keys, values, cotangent)
    outputs = (mixed, grad_query, grad_key, grad_value)

    x, high, core = me // 4, lax.rem(me // 2, 2), lax.rem(me, 2)
    low, y = row // 4, lax.rem(row, 4)
    place = (x * 2 + core) * 4 + y
    depth = high * 4 + low
    planes = gathered.shape[0]
    depths = stacked.shape[0]
    owned = place // tiles
    ahead = jnp.where((low == 0) | (low == 3), OUTER, INNER)

    def in_plane(index):
        return device(
            (index // 8) * 4 + high * 2 + lax.rem(index // 4, 2), low * 4 + lax.rem(index, 4)
        )

    def in_depth(index):
        return device(x * 4 + (index // 4) * 2 + core, lax.rem(index, 4) * 4 + y)

    def remote(source, target, send, recv, where):
        return pltpu.make_async_remote_copy(
            src_ref=source,
            dst_ref=target,
            send_sem=send,
            recv_sem=recv,
            device_id=where,
            device_id_type=MESH,
        )

    def head_copy(n):
        return remote(
            head_out.at[n], head_in.at[n], send_head.at[n], recv_head.at[n], device(after, row)
        )

    main = pl.ds(EDGE, tokens - EDGE)
    half = chunk // 2
    parts = (
        (main, pl.ds(0, half)),
        (pl.ds(0, EDGE), pl.ds(0, chunk)),
        (main, pl.ds(half, half)),
    )

    def u_copy(n, part):
        rows, lanes = parts[part]
        return remote(
            u_own.at[n, rows, lanes], u_prior.at[n, rows, lanes], send_u.at[n, part],
            recv_u.at[n, part], device(after, row),
        )

    def dz_copy(n, part):
        rows, lanes = parts[part]
        return remote(
            dz_own.at[n, rows, lanes], dz_next.at[n, rows, lanes], send_dz.at[n, part],
            recv_dz.at[n, part], device(before, row),
        )

    def send_part(n, part):
        @pl.when(has_next)
        def _():
            u_copy(n, part).start()

        @pl.when(has_prior)
        def _():
            dz_copy(n, part).start()

    def back_copy(n):
        return remote(
            back_out.at[n], back_in.at[n], send_back.at[n], recv_back.at[n], device(before, row)
        )

    def first(peer, slot):
        return remote(
            partial.at[peer], gathered.at[slot], send_one.at[peer], recv_one.at[slot],
            in_plane(peer),
        )

    def second(peer, slot):
        return remote(
            stacked.at[depth], stacked.at[slot], send_two.at[peer], recv_two.at[slot],
            in_depth(peer),
        )

    def third(peer, slot):
        return remote(
            spread_sums.at[place], spread_sums.at[slot], send_three.at[peer],
            recv_three.at[slot], in_plane(peer),
        )

    def load(n, which):
        lanes = pl.ds(pl.multiple_of(n * chunk, chunk), chunk)
        return pltpu.make_async_copy(
            sources[which].at[:, lanes], inputs.at[n, which], load_sem.at[n, which]
        )

    def save(n, which):
        lanes = pl.ds(pl.multiple_of(n * chunk, chunk), chunk)
        rows = pl.ds(0, tokens if which == 0 else tokens - 16)
        return pltpu.make_async_copy(
            results.at[n, which, rows], outputs[which].at[rows, lanes], store_sem.at[n, which]
        )

    def save_tail(n, stream):
        lanes = pl.ds(pl.multiple_of(n * chunk, chunk), chunk)
        rows = pl.ds(tokens - 16, 16)
        return pltpu.make_async_copy(
            results.at[n, 1 + stream, rows],
            outputs[1 + stream].at[rows, lanes],
            tail_sem.at[n, stream],
        )

    def each(size, mine, action):
        for k in range(1, size):
            action(lax.rem(mine + k, size))

    def over(size, action):
        def body(k, carry):
            action(k)
            return carry

        lax.fori_loop(0, size, body, 0)

    def load_all(n):
        for which in (1, 2, 0, 3):
            load(n, which).start()

    over(steps, load_all)

    barrier = pltpu.get_barrier_semaphore()

    def greet(where):
        pl.semaphore_signal(barrier, inc=1, device_id=where, device_id_type=MESH)

    greet(device(after, row))
    greet(device(before, row))
    for k in range(1, planes):
        greet(in_plane(lax.rem(place + k, planes)))
    for k in range(1, depths):
        greet(in_depth(lax.rem(depth + k, depths)))

    starts = [jnp.int32(0)]
    for index in range(lengths.shape[1] - 1):
        starts.append(starts[-1] + lengths[0, index])

    def docs(positions):
        result = jnp.full(positions.shape, -1, jnp.int32)
        for start in starts:
            result = result + (positions >= start).astype(jnp.int32)
        return result

    def iota(shape, dim):
        return lax.broadcasted_iota(jnp.int32, shape, dim)

    anchor = me * tokens
    reach = tokens + 2 * HALO
    places[...] = docs(iota((reach, LANES), 0) + (anchor - HALO))
    own_docs = places[HALO : HALO + tokens]
    for offset in range(1, count_taps):
        prior_docs = places[HALO - offset : HALO - offset + tokens]
        feat_mask[offset - 1] = jnp.where(prior_docs == own_docs, 1.0, 0.0)
    spread = tokens + HALO
    here = iota((spread, LANES), 0) - HALO
    here_docs = places[0:spread]
    for offset in range(count_taps):
        there = here + offset
        fits = (there >= 0) & (there < tokens) & (places[offset : offset + spread] == here_docs)
        back_mask[offset] = jnp.where(fits, 1.0, 0.0)
    wide = (tokens, 2 * tokens)
    across = docs(iota((8, 3 * tokens), 1) + (anchor - tokens))[0:1]
    source_docs = jnp.broadcast_to(across[:, : 2 * tokens], wide)
    target_docs = jnp.broadcast_to(across[:, tokens:], wide)
    down = iota(wide, 0)
    side = iota(wide, 1)
    twice = jnp.concatenate([own_docs, own_docs], 1)
    lag = down - side + tokens
    fits = (twice == source_docs) & (lag >= 0) & (lag < tokens)
    conv_mask[...] = jnp.where(fits, 1.0, 0.0).astype(jnp.bfloat16)
    lag = side - down
    fits = (twice == target_docs) & (lag >= 0) & (lag < tokens)
    du_mask[...] = jnp.where(fits, 1.0, 0.0).astype(jnp.bfloat16)
    turned_docs = docs((anchor + tokens - 1) - iota((tokens, LANES), 0))
    twice = jnp.concatenate([turned_docs, turned_docs], 1)
    lag = 2 * tokens - 1 - down - side
    fits = (twice == source_docs) & (lag >= 0) & (lag < tokens)
    conv_keep[...] = jnp.where(fits, 1.0, 0.0)
    for stream in range(3):
        grads[stream, 0:HALO] = jnp.zeros((HALO, LANES), jnp.float32)
        grads[stream, HALO + tokens :] = jnp.zeros((HALO, LANES), jnp.float32)
    sums[...] = jnp.zeros(sums.shape, jnp.float32)
    packed[...] = jnp.zeros(packed.shape, jnp.float32)

    def clear(tile):
        for stream in range(3):
            window[tile, stream, 0:HALO] = jnp.zeros((HALO, LANES), jnp.float32)

    over(width // LANES, clear)
    lane_group = iota((tokens, LANES), 1) // group_width
    lane_group_twice = jnp.concatenate([lane_group, lane_group], 0)
    square = (LANES, LANES)
    turn = (iota(square, 0) + iota(square, 1)) % LANES == 0
    flipped[...] = jnp.dot(
        filters[...].astype(jnp.bfloat16),
        jnp.where(turn, 1.0, 0.0).astype(jnp.bfloat16),
        preferred_element_type=jnp.float32,
    )
    opposite = iota((tokens, LANES), 0) + iota((tokens, LANES), 1) == tokens - 1
    upside = jnp.where(opposite, 1.0, 0.0).astype(jnp.bfloat16)

    @pl.when(jnp.logical_not(has_prior))
    def _():
        u_prior[...] = jnp.zeros(u_prior.shape, u_prior.dtype)
        head_in[...] = jnp.zeros(head_in.shape, head_in.dtype)

    @pl.when(jnp.logical_not(has_next))
    def _():
        dz_next[...] = jnp.zeros(dz_next.shape, dz_next.dtype)
        back_in[...] = jnp.zeros(back_in.shape, back_in.dtype)

    def spot(i, stream):
        at = (i * 3 + stream) * margin
        return slice(at, at + margin)

    def stage_head(n):
        for which in (1, 2, 0):
            load(n, which).wait()
        for i in range(tiles):
            for stream in range(3):
                last = inputs[n, stream, tokens - 16 : tokens, i * LANES : (i + 1) * LANES]
                packed[spot(i, stream)] = last.astype(jnp.float32)[16 - margin :]
        head_out[n] = packed[...].astype(jnp.bfloat16)

    def send_head_on(n):
        @pl.when(has_next)
        def _():
            head_copy(n).start()

    def open_heads(n):
        packed[...] = head_in[n].astype(jnp.float32)
        for i in range(tiles):
            for stream in range(3):
                window[n * tiles + i, stream, HALO - margin : HALO] = packed[spot(i, stream)]

    def featurize(n, i):
        tile = n * tiles + i
        lanes = pl.ds(pl.multiple_of(tile * LANES, LANES), LANES)
        inner = pl.ds(pl.multiple_of(i * LANES, LANES), LANES)
        made = []
        for stream in range(3):
            own = inputs[n, stream, :, inner].astype(jnp.float32)
            window[tile, stream, HALO : HALO + tokens] = own
            own = own[EDGE:]
            result = taps[stream, 0:1, lanes] * own
            for offset in range(1, count_taps):
                start = HALO + EDGE - offset
                shifted = window[tile, stream, start : start + tokens - EDGE]
                result = result + taps[stream, offset : offset + 1, lanes] * (
                    shifted * feat_mask[offset - 1, EDGE:]
                )
            feats[tile, stream, EDGE:] = result
            made.append(result)
        u_own[n, EDGE:, inner] = (made[1] * made[2]).astype(jnp.bfloat16)
        gradient = inputs[n, 3, EDGE:, inner].astype(jnp.float32)
        dz_own[n, EDGE:, inner] = (gradient * made[0]).astype(jnp.bfloat16)

    def refine(n, i):
        tile = n * tiles + i
        lanes = pl.ds(pl.multiple_of(tile * LANES, LANES), LANES)
        inner = pl.ds(pl.multiple_of(i * LANES, LANES), LANES)
        made = []
        for stream in range(3):
            result = taps[stream, 0:1, lanes] * window[tile, stream, HALO : HALO + EDGE]
            for offset in range(1, count_taps):
                start = HALO - offset
                shifted = window[tile, stream, start : start + EDGE]
                result = result + taps[stream, offset : offset + 1, lanes] * (
                    shifted * feat_mask[offset - 1, 0:EDGE]
                )
            feats[tile, stream, 0:EDGE] = result
            made.append(result)
        u_own[n, 0:EDGE, inner] = (made[1] * made[2]).astype(jnp.bfloat16)
        gradient = inputs[n, 3, 0:EDGE, inner].astype(jnp.float32)
        dz_own[n, 0:EDGE, inner] = (gradient * made[0]).astype(jnp.bfloat16)

    def convolve(n, i):
        tile = n * tiles + i
        lanes = pl.ds(pl.multiple_of(tile * LANES, LANES), LANES)
        inner = pl.ds(pl.multiple_of(i * LANES, LANES), LANES)
        u_tile = u_own[n, :, inner]
        dz_tile = dz_own[n, :, inner]
        dz_turned = jnp.dot(upside, dz_tile, preferred_element_type=jnp.float32)
        dz_turned = dz_turned.astype(jnp.bfloat16)
        u_window = jnp.concatenate([u_prior[n, :, inner], u_tile], 0)
        dz_window = jnp.concatenate([dz_tile, dz_next[n, :, inner]], 0)
        zero = jnp.zeros((), jnp.bfloat16)
        rows = pl.ds(pl.multiple_of(tile * per_tile, per_tile), per_tile)
        own_taps, own_flipped = filters[rows], flipped[rows]

        def circulant(line, mask):
            turned = jnp.broadcast_to(line, (tokens, LANES))
            turned = pltpu.roll(turned, 0, 1, stride=1, stride_axis=0).astype(jnp.bfloat16)
            return jnp.concatenate([turned, turned], 1) * mask[...]

        def pick(group, value):
            picks = lane_group if value.shape[0] == tokens else lane_group_twice
            return jnp.where(picks == group, value, zero)

        def convolved(lines, mask, value):
            left = [circulant(lines[g : g + 1], mask) for g in range(per_tile)]
            right = [pick(g, value) for g in range(per_tile)]
            return jnp.dot(
                jnp.concatenate(left, 1),
                jnp.concatenate(right, 0),
                preferred_element_type=jnp.float32,
            )

        conv = convolved(own_flipped, conv_mask, u_window)
        du = convolved(own_taps, du_mask, dz_window)
        for group in range(per_tile):
            outer = lax.dot_general(
                pick(group, dz_turned),
                u_window,
                (((1,), (1,)), ((), ())),
                preferred_element_type=jnp.float32,
            )
            outer = outer * conv_keep[...]
            folded = outer[:, :LANES] + outer[:, LANES:]
            turned = pltpu.roll(folded, 0, 1, stride=1, stride_axis=0)
            sums[24 + group : 25 + group] = jnp.sum(turned, axis=0, keepdims=True)
        u_float = u_tile.astype(jnp.float32)
        gradient = inputs[n, 3, :, inner].astype(jnp.float32)
        gain = skip[:, lanes]
        q_feat = feats[tile, 0]
        dz = gradient * q_feat
        total = conv + gain * u_float
        results[n, 0, :, inner] = (q_feat * total).astype(jnp.bfloat16)
        sums[count_taps : count_taps + 1] = jnp.sum(dz * u_float, axis=0, keepdims=True)
        du = du + gain * dz
        inside = pl.ds(HALO, tokens)
        grads[0, inside] = gradient * total
        grads[1, inside] = du * feats[tile, 2]
        grads[2, inside] = du * feats[tile, 1]
        for stream in range(3):
            result = None
            x_window = window[tile, stream]
            for offset in range(count_taps):
                shifted = grads[stream, offset : offset + tokens + HALO] * back_mask[offset]
                term = taps[stream, offset : offset + 1, lanes] * shifted
                result = term if result is None else result + term
                line = stream * 8 + offset
                sums[line : line + 1] = jnp.sum(shifted * x_window, axis=0, keepdims=True)
            heads[i, stream] = result[:HALO]
            tails[stream, :, lanes] = result[HALO + tokens - 16 :]
            whole = result[HALO : HALO + tokens - 16]
            results[n, 1 + stream, 0 : tokens - 16, inner] = whole.astype(jnp.bfloat16)
        partial[tile] = sums[...].astype(jnp.bfloat16)

        @pl.when(tile != place)
        def _():
            first(tile, place).start()

    def gather_own():
        gathered[place] = partial[place]
        each(planes, place, lambda peer: first(peer, peer).wait_recv())
        total = gathered[0].astype(jnp.float32)
        for index in range(1, planes):
            total = total + gathered[index].astype(jnp.float32)
        stacked[depth] = total.astype(jnp.bfloat16)
        each(depths, depth, lambda peer: second(peer, depth).start())

    def spread_own():
        each(depths, depth, lambda peer: second(peer, peer).wait_recv())
        total = stacked[0].astype(jnp.float32)
        for index in range(1, depths):
            total = total + stacked[index].astype(jnp.float32)
        spread_sums[place] = (total * scale).astype(jnp.bfloat16)
        each(planes, place, lambda peer: third(peer, place).start())

    def prepare(n):
        load(n, 3).wait()
        over(tiles, lambda i: featurize(n, i))

    over(LEAD, stage_head)
    over(EARLY, prepare)
    pl.semaphore_wait(barrier, planes + depths)
    over(LEAD, send_head_on)

    def step(n):
        @pl.when(n + LEAD < steps)
        def _():
            stage_head(n + LEAD)
            send_head_on(n + LEAD)

        @pl.when(n < steps)
        def _():
            @pl.when(n >= EARLY)
            def _():
                prepare(n)

            send_part(n, 0)
            send_part(n, 2)

        ready = n - REFINE

        @pl.when((ready >= 0) & (ready < steps))
        def _():
            @pl.when(has_prior)
            def _():
                head_copy(ready).wait_recv()

            open_heads(ready)
            over(tiles, lambda i: refine(ready, i))
            send_part(ready, 1)

        past = n - ahead

        @pl.when((past >= 0) & (past < steps))
        def _():
            @pl.when(has_prior)
            def _():
                u_copy(past, 0).wait_recv()
                u_copy(past, 1).wait_recv()

            @pl.when(has_next)
            def _():
                dz_copy(past, 0).wait_recv()
                dz_copy(past, 1).wait_recv()

            def one(i):
                @pl.when((i == tiles // 2) & has_prior)
                def _():
                    u_copy(past, 2).wait_recv()

                @pl.when((i == tiles // 2) & has_next)
                def _():
                    dz_copy(past, 2).wait_recv()

                convolve(past, i)

            over(tiles, one)
            packed[...] = jnp.zeros(packed.shape, jnp.float32)
            for i in range(tiles):
                for stream in range(3):
                    packed[spot(i, stream)] = heads[i, stream, HALO - margin : HALO]
            back_out[past] = packed[...].astype(jnp.bfloat16)

            for which in range(4):
                save(past, which).start()

            @pl.when(past == owned + 2)
            def _():
                gather_own()

            @pl.when(past == owned + 3)
            def _():
                spread_own()

    over(steps + max(OUTER, INNER), step)

    @pl.when(owned >= steps - 2)
    def _():
        gather_own()

    @pl.when(has_prior)
    def _():
        over(steps, lambda n: back_copy(n).start())

    @pl.when(owned >= steps - 3)
    def _():
        spread_own()

    def settle(n):
        @pl.when(has_next)
        def _():
            back_copy(n).wait_recv()

        packed[...] = back_in[n].astype(jnp.float32)
        for i in range(tiles):
            lanes = pl.ds(pl.multiple_of(n * chunk + i * LANES, LANES), LANES)
            for stream in range(3):
                tails[stream, 16 - margin : 16, lanes] += packed[spot(i, stream)]
                fixed = tails[stream, :, lanes].astype(jnp.bfloat16)
                results[n, 1 + stream, tokens - 16 : tokens, i * LANES : (i + 1) * LANES] = fixed
        for stream in range(3):
            save_tail(n, stream).start()

    def drain(n):
        for which in range(4):
            save(n, which).wait()
        for stream in range(3):
            save_tail(n, stream).wait()

        @pl.when(has_next)
        def _():
            head_copy(n).wait_send()
            u_copy(n, 0).wait_send()
            u_copy(n, 1).wait_send()
            u_copy(n, 2).wait_send()

        @pl.when(has_prior)
        def _():
            dz_copy(n, 0).wait_send()
            dz_copy(n, 1).wait_send()
            dz_copy(n, 2).wait_send()
            back_copy(n).wait_send()

    over(steps, settle)
    over(steps, drain)
    each(planes, place, lambda peer: first(peer, place).wait_send())
    each(depths, depth, lambda peer: second(peer, depth).wait_send())
    each(planes, place, lambda peer: third(peer, place).wait_send())
    each(planes, place, lambda peer: third(peer, peer).wait_recv())


def finish_kernel(
    mixed_in,
    query_in,
    key_in,
    value_in,
    sums_in,
    mixed,
    grad_query,
    grad_key,
    grad_value,
    short_out,
    filters_out,
    skip_out,
    sums,
    short,
    filters,
    skip,
    opened,
    stage,
    loaded,
    copied,
    other,
):
    pairs = (mixed_in, mixed), (query_in, grad_query), (key_in, grad_key), (value_in, grad_value)
    parts = copied.shape[1]
    half = mixed.shape[0] // parts
    loads, saves = [], []
    for index, (given, out) in enumerate(pairs):
        for part in range(parts):
            rows = pl.ds(part * half, half)
            here = stage.at[index, rows]
            loads.append(pltpu.make_async_copy(given.at[rows], here, loaded.at[index, part]))
            saves.append(pltpu.make_async_copy(here, out.at[rows], copied.at[index, part]))
    first = pltpu.make_async_copy(sums_in, sums, other.at[0])
    first.start()
    for copy in loads:
        copy.start()
    tiles = sums.shape[0]
    count_taps = short.shape[1]
    per_tile = filters.shape[0] // tiles
    square = (LANES, LANES)
    turn = lax.broadcasted_iota(jnp.int32, square, 0) + lax.broadcasted_iota(jnp.int32, square, 1)
    turn = jnp.where(turn == LANES - 1, 1.0, 0.0).astype(jnp.bfloat16)

    first.wait()
    for i in range(tiles):
        lanes = slice(i * LANES, (i + 1) * LANES)
        opened[i] = sums[i].astype(jnp.float32)
        for stream in range(3):
            short[stream, :, lanes] = opened[i, stream * 8 : stream * 8 + count_taps]
        skip[:, lanes] = opened[i, count_taps : count_taps + 1]
        filters[i * per_tile : (i + 1) * per_tile] = jnp.dot(
            opened[i, 24:].astype(jnp.bfloat16), turn, preferred_element_type=jnp.float32
        )
    pieces = ((short, short_out), (filters, filters_out), (skip, skip_out))
    for index, (given, out) in enumerate(pieces):
        saves.append(pltpu.make_async_copy(given, out, other.at[1 + index]))
        saves[-1].start()
    for coming, leaving in zip(loads, saves):
        coming.wait()
        leaving.start()
    for copy in saves:
        copy.wait()


def local_block(scale, query, keys, values, cotangent, taps, filters, skip, lengths):
    steps = STEPS
    tokens, width = query.shape
    groups = filters.shape[0]
    chunk = width // steps
    tiles = width // LANES
    count_taps = taps.shape[1]
    spots = -(-3 * (count_taps - 1) * (chunk // LANES) // 16) * 16
    bf16, f32 = jnp.bfloat16, jnp.float32
    stream = jax.ShapeDtypeStruct((tokens, width), bf16)
    vmem = pl.BlockSpec(memory_space=pltpu.VMEM)
    hbm = pl.BlockSpec(memory_space=pl.ANY)
    dma = pltpu.SemaphoreType.DMA((steps,))
    pair = pltpu.SemaphoreType.DMA((steps, 3))
    plane = pltpu.SemaphoreType.DMA((32,))
    depth = pltpu.SemaphoreType.DMA((8,))
    piece = pltpu.VMEM((steps, tokens, chunk), bf16)
    margin = pltpu.VMEM((steps, spots, LANES), bf16)
    made = pl.pallas_call(
        functools.partial(block_kernel, steps, width // groups, scale),
        out_shape=[stream] * 4
        + [jax.ShapeDtypeStruct((tiles, 32, LANES), bf16)],
        in_specs=[pl.BlockSpec(memory_space=pltpu.SMEM)] + [hbm] * 4 + [vmem] * 3,
        out_specs=[hbm] * 4 + [vmem],
        scratch_shapes=[
            pltpu.VMEM((steps, 4, tokens, chunk), bf16),
            pltpu.VMEM((steps, 4, tokens, chunk), bf16),
            pltpu.VMEM((3, 16, width), f32),
            pltpu.VMEM((tiles, 3, tokens + HALO, LANES), f32),
            pltpu.VMEM((tiles, 3, tokens, LANES), f32),
            pltpu.VMEM((groups, LANES), f32),
            piece,
            piece,
            piece,
            piece,
            margin,
            margin,
            margin,
            margin,
            pltpu.VMEM((chunk // LANES, 3, HALO, LANES), f32),
            pltpu.VMEM((spots, LANES), f32),
            pltpu.VMEM((tokens + 2 * HALO, LANES), jnp.int32),
            pltpu.VMEM((count_taps - 1, tokens, LANES), f32),
            pltpu.VMEM((count_taps, tokens + HALO, LANES), f32),
            pltpu.VMEM((tokens, 2 * tokens), bf16),
            pltpu.VMEM((tokens, 2 * tokens), f32),
            pltpu.VMEM((tokens, 2 * tokens), bf16),
            pltpu.VMEM((3, tokens + 2 * HALO, LANES), f32),
            pltpu.VMEM((32, LANES), f32),
            pltpu.VMEM((tiles, 32, LANES), bf16),
            pltpu.VMEM((32, 32, LANES), bf16),
            pltpu.VMEM((8, 32, LANES), bf16),
            pltpu.SemaphoreType.DMA((steps, 4)),
            pltpu.SemaphoreType.DMA((steps, 4)),
            pltpu.SemaphoreType.DMA((steps, 3)),
        ]
        + [pair] * 4
        + [dma] * 4
        + [plane, plane, depth, depth, plane, plane],
        compiler_params=pltpu.CompilerParams(
            collective_id=0, has_side_effects=True, vmem_limit_bytes=56 * 2**20
        ),
        name="block",
    )(lengths, query, keys, values, cotangent, taps, filters, skip)
    return pl.pallas_call(
        finish_kernel,
        out_shape=[stream] * 4
        + [
            jax.ShapeDtypeStruct(taps.shape, f32),
            jax.ShapeDtypeStruct(filters.shape, f32),
            jax.ShapeDtypeStruct(skip.shape, f32),
        ],
        in_specs=[hbm] * 5,
        out_specs=[hbm] * 7,
        scratch_shapes=[
            pltpu.VMEM((tiles, 32, LANES), bf16),
            pltpu.VMEM(taps.shape, f32),
            pltpu.VMEM(filters.shape, f32),
            pltpu.VMEM(skip.shape, f32),
            pltpu.VMEM((tiles, 32, LANES), f32),
            pltpu.VMEM((4, tokens, width), bf16),
            pltpu.SemaphoreType.DMA((4, 4)),
            pltpu.SemaphoreType.DMA((4, 4)),
            pltpu.SemaphoreType.DMA((4,)),
        ],
        compiler_params=pltpu.CompilerParams(vmem_limit_bytes=60 * 2**20),
        name="finish",
    )(*made)


def shards(
    query_proj, key_proj, value_proj, short_taps, filter_taps, skip_gain, doc_lengths, out_grad
):
    tokens = query_proj.shape[1]
    scale = 1.0 / math.sqrt(tokens * lax.axis_size("ctx") * lax.axis_size("dp"))
    mixed, grad_query, grad_key, grad_value, short, filters, gain = local_block(
        scale,
        query_proj[0],
        key_proj[0],
        value_proj[0],
        out_grad[0],
        short_taps,
        filter_taps,
        skip_gain[None],
        doc_lengths,
    )
    return (
        mixed[None],
        grad_query[None],
        grad_key[None],
        grad_value[None],
        short,
        filters,
        gain[0],
    )


def solution(mesh):
    return jax.shard_map(
        shards,
        mesh=mesh,
        in_specs=(
            P("dp", "ctx", None),
            P("dp", "ctx", None),
            P("dp", "ctx", None),
            P(),
            P(),
            P(),
            P("dp", None),
            P("dp", "ctx", None),
        ),
        out_specs=(
            P("dp", "ctx", None),
            P("dp", "ctx", None),
            P("dp", "ctx", None),
            P("dp", "ctx", None),
            P(),
            P(),
            P(),
        ),
        check_vma=False,
    )
```

```python
import functools
import math

import jax
import jax.numpy as jnp
from jax import lax
from jax.experimental import pallas as pl
from jax.experimental.pallas import tpu as pltpu
from jax.sharding import PartitionSpec as P

MESH = pl.DeviceIdType.MESH
LANES = 128
HALO = 8
STEPS = 8
OUTER, INNER = 3, 4
LEAD = 2
EARLY = 2
EDGE = 16
REFINE = 1


def device(ctx, dp):
    return {"ctx": ctx, "dp": dp}


def block_kernel(
    steps,
    group_width,
    scale,
    lengths,
    query,
    keys,
    values,
    cotangent,
    taps_in,
    filters_in,
    skip_in,
    mixed,
    grad_query,
    grad_key,
    grad_value,
    spread_sums,
    taps,
    filters,
    skip,
    param_sem,
    inputs,
    results,
    tails,
    window,
    feats,
    flipped,
    u_own,
    dz_own,
    u_prior,
    dz_next,
    head_out,
    head_in,
    back_out,
    back_in,
    heads,
    packed,
    places,
    feat_mask,
    back_mask,
    conv_mask,
    conv_keep,
    du_mask,
    grads,
    sums,
    partial,
    gathered,
    stacked,
    load_sem,
    store_sem,
    tail_sem,
    send_u,
    recv_u,
    send_dz,
    recv_dz,
    send_head,
    recv_head,
    send_back,
    recv_back,
    send_one,
    recv_one,
    send_two,
    recv_two,
    send_three,
    recv_three,
):
    me = lax.axis_index("ctx")
    row = lax.axis_index("dp")
    count = lax.axis_size("ctx")
    after, before = lax.rem(me + 1, count), lax.rem(me + count - 1, count)
    tokens, width = query.shape
    chunk = width // steps
    tiles = chunk // LANES
    count_taps = taps.shape[1]
    margin = count_taps - 1
    per_tile = LANES // group_width
    has_prior, has_next = me > 0, me < count - 1
    sources = (query, keys, values, cotangent)
    outputs = (mixed, grad_query, grad_key, grad_value)

    x, high, core = me // 4, lax.rem(me // 2, 2), lax.rem(me, 2)
    low, y = row // 4, lax.rem(row, 4)
    place = (x * 2 + core) * 4 + y
    depth = high * 4 + low
    planes = gathered.shape[0]
    depths = stacked.shape[0]
    owned = place // tiles
    ahead = jnp.where((low == 0) | (low == 3), OUTER, INNER)

    def in_plane(index):
        return device(
            (index // 8) * 4 + high * 2 + lax.rem(index // 4, 2), low * 4 + lax.rem(index, 4)
        )

    def in_depth(index):
        return device(x * 4 + (index // 4) * 2 + core, lax.rem(index, 4) * 4 + y)

    def remote(source, target, send, recv, where):
        return pltpu.make_async_remote_copy(
            src_ref=source,
            dst_ref=target,
            send_sem=send,
            recv_sem=recv,
            device_id=where,
            device_id_type=MESH,
        )

    def head_copy(n):
        return remote(
            head_out.at[n], head_in.at[n], send_head.at[n], recv_head.at[n], device(after, row)
        )

    main = pl.ds(EDGE, tokens - EDGE)
    half = chunk // 2
    parts = (
        (main, pl.ds(0, half)),
        (pl.ds(0, EDGE), pl.ds(0, chunk)),
        (main, pl.ds(half, half)),
    )

    def u_copy(n, part):
        rows, lanes = parts[part]
        return remote(
            u_own.at[n, rows, lanes], u_prior.at[n, rows, lanes], send_u.at[n, part],
            recv_u.at[n, part], device(after, row),
        )

    def dz_copy(n, part):
        rows, lanes = parts[part]
        return remote(
            dz_own.at[n, rows, lanes], dz_next.at[n, rows, lanes], send_dz.at[n, part],
            recv_dz.at[n, part], device(before, row),
        )

    def send_part(n, part):
        @pl.when(has_next)
        def _():
            u_copy(n, part).start()

        @pl.when(has_prior)
        def _():
            dz_copy(n, part).start()

    def back_copy(n):
        return remote(
            back_out.at[n], back_in.at[n], send_back.at[n], recv_back.at[n], device(before, row)
        )

    def first(peer, slot):
        return remote(
            partial.at[peer], gathered.at[slot], send_one.at[peer], recv_one.at[slot],
            in_plane(peer),
        )

    def second(peer, slot):
        return remote(
            stacked.at[depth], stacked.at[slot], send_two.at[peer], recv_two.at[slot],
            in_depth(peer),
        )

    def third(peer, slot):
        return remote(
            spread_sums.at[place], spread_sums.at[slot], send_three.at[peer],
            recv_three.at[slot], in_plane(peer),
        )

    def load(n, which):
        lanes = pl.ds(pl.multiple_of(n * chunk, chunk), chunk)
        return pltpu.make_async_copy(
            sources[which].at[:, lanes], inputs.at[n, which], load_sem.at[n, which]
        )

    def save(n, which):
        lanes = pl.ds(pl.multiple_of(n * chunk, chunk), chunk)
        rows = pl.ds(0, tokens if which == 0 else tokens - 16)
        return pltpu.make_async_copy(
            results.at[n, which, rows], outputs[which].at[rows, lanes], store_sem.at[n, which]
        )

    def save_tail(n, stream):
        lanes = pl.ds(pl.multiple_of(n * chunk, chunk), chunk)
        rows = pl.ds(tokens - 16, 16)
        return pltpu.make_async_copy(
            results.at[n, 1 + stream, rows],
            outputs[1 + stream].at[rows, lanes],
            tail_sem.at[n, stream],
        )

    def each(size, mine, action):
        for k in range(1, size):
            action(lax.rem(mine + k, size))

    def over(size, action):
        def body(k, carry):
            action(k)
            return carry

        lax.fori_loop(0, size, body, 0)

    def load_all(n):
        for which in (1, 2, 0, 3):
            load(n, which).start()

    params = [
        pltpu.make_async_copy(given, held, param_sem.at[index])
        for index, (given, held) in enumerate(
            ((taps_in, taps), (filters_in, filters), (skip_in, skip))
        )
    ]

    barrier = pltpu.get_barrier_semaphore()

    def greet(where):
        pl.semaphore_signal(barrier, inc=1, device_id=where, device_id_type=MESH)

    greet(device(after, row))
    greet(device(before, row))
    for k in range(1, planes):
        greet(in_plane(lax.rem(place + k, planes)))
    for k in range(1, depths):
        greet(in_depth(lax.rem(depth + k, depths)))

    for copy in params:
        copy.start()
    over(steps, load_all)
    starts = [jnp.int32(0)]
    for index in range(lengths.shape[1] - 1):
        starts.append(starts[-1] + lengths[0, index])

    def docs(positions):
        result = jnp.full(positions.shape, -1, jnp.int32)
        for start in starts:
            result = result + (positions >= start).astype(jnp.int32)
        return result

    def iota(shape, dim):
        return lax.broadcasted_iota(jnp.int32, shape, dim)

    anchor = me * tokens
    reach = tokens + 2 * HALO
    places[...] = docs(iota((reach, LANES), 0) + (anchor - HALO))
    own_docs = places[HALO : HALO + tokens]
    for offset in range(1, count_taps):
        prior_docs = places[HALO - offset : HALO - offset + tokens]
        feat_mask[offset - 1] = jnp.where(prior_docs == own_docs, 1.0, 0.0)
    spread = tokens + HALO
    here = iota((spread, LANES), 0) - HALO
    here_docs = places[0:spread]
    for offset in range(count_taps):
        there = here + offset
        fits = (there >= 0) & (there < tokens) & (places[offset : offset + spread] == here_docs)
        back_mask[offset] = jnp.where(fits, 1.0, 0.0)
    wide = (tokens, 2 * tokens)
    across = docs(iota((8, 3 * tokens), 1) + (anchor - tokens))[0:1]
    source_docs = jnp.broadcast_to(across[:, : 2 * tokens], wide)
    target_docs = jnp.broadcast_to(across[:, tokens:], wide)
    down = iota(wide, 0)
    side = iota(wide, 1)
    twice = jnp.concatenate([own_docs, own_docs], 1)
    lag = down - side + tokens
    fits = (twice == source_docs) & (lag >= 0) & (lag < tokens)
    conv_mask[...] = jnp.where(fits, 1.0, 0.0).astype(jnp.bfloat16)
    lag = side - down
    fits = (twice == target_docs) & (lag >= 0) & (lag < tokens)
    du_mask[...] = jnp.where(fits, 1.0, 0.0).astype(jnp.bfloat16)
    turned_docs = docs((anchor + tokens - 1) - iota((tokens, LANES), 0))
    twice = jnp.concatenate([turned_docs, turned_docs], 1)
    lag = 2 * tokens - 1 - down - side
    fits = (twice == source_docs) & (lag >= 0) & (lag < tokens)
    conv_keep[...] = jnp.where(fits, 1.0, 0.0)
    for stream in range(3):
        grads[stream, 0:HALO] = jnp.zeros((HALO, LANES), jnp.float32)
        grads[stream, HALO + tokens :] = jnp.zeros((HALO, LANES), jnp.float32)
    sums[...] = jnp.zeros(sums.shape, jnp.float32)
    packed[...] = jnp.zeros(packed.shape, jnp.float32)

    def clear(tile):
        for stream in range(3):
            window[tile, stream, 0:HALO] = jnp.zeros((HALO, LANES), jnp.float32)

    over(width // LANES, clear)
    lane_group = iota((tokens, LANES), 1) // group_width
    lane_group_twice = jnp.concatenate([lane_group, lane_group], 0)
    square = (LANES, LANES)
    turn = (iota(square, 0) + iota(square, 1)) % LANES == 0
    for copy in params:
        copy.wait()
    flipped[...] = jnp.dot(
        filters[...].astype(jnp.bfloat16),
        jnp.where(turn, 1.0, 0.0).astype(jnp.bfloat16),
        preferred_element_type=jnp.float32,
    )
    opposite = iota((tokens, LANES), 0) + iota((tokens, LANES), 1) == tokens - 1
    upside = jnp.where(opposite, 1.0, 0.0).astype(jnp.bfloat16)

    @pl.when(jnp.logical_not(has_prior))
    def _():
        u_prior[...] = jnp.zeros(u_prior.shape, u_prior.dtype)
        head_in[...] = jnp.zeros(head_in.shape, head_in.dtype)

    @pl.when(jnp.logical_not(has_next))
    def _():
        dz_next[...] = jnp.zeros(dz_next.shape, dz_next.dtype)
        back_in[...] = jnp.zeros(back_in.shape, back_in.dtype)

    def spot(i, stream):
        at = (i * 3 + stream) * margin
        return slice(at, at + margin)

    def stage_head(n):
        for which in (1, 2, 0):
            load(n, which).wait()
        for i in range(tiles):
            for stream in range(3):
                last = inputs[n, stream, tokens - 16 : tokens, i * LANES : (i + 1) * LANES]
                packed[spot(i, stream)] = last.astype(jnp.float32)[16 - margin :]
        head_out[n] = packed[...].astype(jnp.bfloat16)

    def send_head_on(n):
        @pl.when(has_next)
        def _():
            head_copy(n).start()

    def open_heads(n):
        packed[...] = head_in[n].astype(jnp.float32)
        for i in range(tiles):
            for stream in range(3):
                window[n * tiles + i, stream, HALO - margin : HALO] = packed[spot(i, stream)]

    def featurize(n, i):
        tile = n * tiles + i
        lanes = pl.ds(pl.multiple_of(tile * LANES, LANES), LANES)
        inner = pl.ds(pl.multiple_of(i * LANES, LANES), LANES)
        made = []
        for stream in range(3):
            own = inputs[n, stream, :, inner].astype(jnp.float32)
            window[tile, stream, HALO : HALO + tokens] = own
            own = own[EDGE:]
            result = taps[stream, 0:1, lanes] * own
            for offset in range(1, count_taps):
                start = HALO + EDGE - offset
                shifted = window[tile, stream, start : start + tokens - EDGE]
                result = result + taps[stream, offset : offset + 1, lanes] * (
                    shifted * feat_mask[offset - 1, EDGE:]
                )
            feats[tile, stream, EDGE:] = result
            made.append(result)
        u_own[n, EDGE:, inner] = (made[1] * made[2]).astype(jnp.bfloat16)
        gradient = inputs[n, 3, EDGE:, inner].astype(jnp.float32)
        dz_own[n, EDGE:, inner] = (gradient * made[0]).astype(jnp.bfloat16)

    def refine(n, i):
        tile = n * tiles + i
        lanes = pl.ds(pl.multiple_of(tile * LANES, LANES), LANES)
        inner = pl.ds(pl.multiple_of(i * LANES, LANES), LANES)
        made = []
        for stream in range(3):
            result = taps[stream, 0:1, lanes] * window[tile, stream, HALO : HALO + EDGE]
            for offset in range(1, count_taps):
                start = HALO - offset
                shifted = window[tile, stream, start : start + EDGE]
                result = result + taps[stream, offset : offset + 1, lanes] * (
                    shifted * feat_mask[offset - 1, 0:EDGE]
                )
            feats[tile, stream, 0:EDGE] = result
            made.append(result)
        u_own[n, 0:EDGE, inner] = (made[1] * made[2]).astype(jnp.bfloat16)
        gradient = inputs[n, 3, 0:EDGE, inner].astype(jnp.float32)
        dz_own[n, 0:EDGE, inner] = (gradient * made[0]).astype(jnp.bfloat16)

    def convolve(n, i):
        tile = n * tiles + i
        lanes = pl.ds(pl.multiple_of(tile * LANES, LANES), LANES)
        inner = pl.ds(pl.multiple_of(i * LANES, LANES), LANES)
        u_tile = u_own[n, :, inner]
        dz_tile = dz_own[n, :, inner]
        dz_turned = jnp.dot(upside, dz_tile, preferred_element_type=jnp.float32)
        dz_turned = dz_turned.astype(jnp.bfloat16)
        u_window = jnp.concatenate([u_prior[n, :, inner], u_tile], 0)
        dz_window = jnp.concatenate([dz_tile, dz_next[n, :, inner]], 0)
        zero = jnp.zeros((), jnp.bfloat16)
        rows = pl.ds(pl.multiple_of(tile * per_tile, per_tile), per_tile)
        own_taps, own_flipped = filters[rows], flipped[rows]

        def circulant(line, mask):
            turned = jnp.broadcast_to(line, (tokens, LANES))
            turned = pltpu.roll(turned, 0, 1, stride=1, stride_axis=0).astype(jnp.bfloat16)
            return jnp.concatenate([turned, turned], 1) * mask[...]

        def pick(group, value):
            picks = lane_group if value.shape[0] == tokens else lane_group_twice
            return jnp.where(picks == group, value, zero)

        def convolved(lines, mask, value):
            left = [circulant(lines[g : g + 1], mask) for g in range(per_tile)]
            right = [pick(g, value) for g in range(per_tile)]
            return jnp.dot(
                jnp.concatenate(left, 1),
                jnp.concatenate(right, 0),
                preferred_element_type=jnp.float32,
            )

        conv = convolved(own_flipped, conv_mask, u_window)
        du = convolved(own_taps, du_mask, dz_window)
        for group in range(per_tile):
            outer = lax.dot_general(
                pick(group, dz_turned),
                u_window,
                (((1,), (1,)), ((), ())),
                preferred_element_type=jnp.float32,
            )
            outer = outer * conv_keep[...]
            folded = outer[:, :LANES] + outer[:, LANES:]
            turned = pltpu.roll(folded, 0, 1, stride=1, stride_axis=0)
            sums[24 + group : 25 + group] = jnp.sum(turned, axis=0, keepdims=True)
        u_float = u_tile.astype(jnp.float32)
        gradient = inputs[n, 3, :, inner].astype(jnp.float32)
        gain = skip[:, lanes]
        q_feat = feats[tile, 0]
        dz = gradient * q_feat
        total = conv + gain * u_float
        results[n, 0, :, inner] = (q_feat * total).astype(jnp.bfloat16)
        sums[count_taps : count_taps + 1] = jnp.sum(dz * u_float, axis=0, keepdims=True)
        du = du + gain * dz
        inside = pl.ds(HALO, tokens)
        grads[0, inside] = gradient * total
        grads[1, inside] = du * feats[tile, 2]
        grads[2, inside] = du * feats[tile, 1]
        for stream in range(3):
            result = None
            x_window = window[tile, stream]
            for offset in range(count_taps):
                shifted = grads[stream, offset : offset + tokens + HALO]
                if offset:
                    shifted = shifted * back_mask[offset]
                term = taps[stream, offset : offset + 1, lanes] * shifted
                result = term if result is None else result + term
                line = stream * 8 + offset
                sums[line : line + 1] = jnp.sum(shifted * x_window, axis=0, keepdims=True)
            heads[i, stream] = result[:HALO]
            tails[stream, :, lanes] = result[HALO + tokens - 16 :]
            whole = result[HALO : HALO + tokens - 16]
            results[n, 1 + stream, 0 : tokens - 16, inner] = whole.astype(jnp.bfloat16)
        partial[tile] = sums[...].astype(jnp.bfloat16)

        @pl.when(tile != place)
        def _():
            first(tile, place).start()

    def gather_own():
        gathered[place] = partial[place]
        each(planes, place, lambda peer: first(peer, peer).wait_recv())
        total = gathered[0].astype(jnp.float32)
        for index in range(1, planes):
            total = total + gathered[index].astype(jnp.float32)
        stacked[depth] = total.astype(jnp.bfloat16)
        each(depths, depth, lambda peer: second(peer, depth).start())

    def spread_own():
        each(depths, depth, lambda peer: second(peer, peer).wait_recv())
        total = stacked[0].astype(jnp.float32)
        for index in range(1, depths):
            total = total + stacked[index].astype(jnp.float32)
        spread_sums[place] = (total * scale).astype(jnp.bfloat16)
        each(planes, place, lambda peer: third(peer, place).start())

    def prepare(n):
        load(n, 3).wait()
        over(tiles, lambda i: featurize(n, i))

    over(LEAD, stage_head)
    over(EARLY, prepare)
    pl.semaphore_wait(barrier, planes + depths)
    over(LEAD, send_head_on)

    def step(n):
        @pl.when(n + LEAD < steps)
        def _():
            stage_head(n + LEAD)
            send_head_on(n + LEAD)

        @pl.when(n < steps)
        def _():
            @pl.when(n >= EARLY)
            def _():
                prepare(n)

            send_part(n, 0)
            send_part(n, 2)

        ready = n - REFINE

        @pl.when((ready >= 0) & (ready < steps))
        def _():
            @pl.when(has_prior)
            def _():
                head_copy(ready).wait_recv()

            open_heads(ready)
            over(tiles, lambda i: refine(ready, i))
            send_part(ready, 1)

        past = n - ahead

        @pl.when((past >= 0) & (past < steps))
        def _():
            @pl.when(has_prior)
            def _():
                u_copy(past, 0).wait_recv()
                u_copy(past, 1).wait_recv()

            @pl.when(has_next)
            def _():
                dz_copy(past, 0).wait_recv()
                dz_copy(past, 1).wait_recv()

            def one(i):
                @pl.when((i == tiles // 2) & has_prior)
                def _():
                    u_copy(past, 2).wait_recv()

                @pl.when((i == tiles // 2) & has_next)
                def _():
                    dz_copy(past, 2).wait_recv()

                convolve(past, i)

            over(tiles, one)
            packed[...] = jnp.zeros(packed.shape, jnp.float32)
            for i in range(tiles):
                for stream in range(3):
                    packed[spot(i, stream)] = heads[i, stream, HALO - margin : HALO]
            back_out[past] = packed[...].astype(jnp.bfloat16)

            for which in range(4):
                save(past, which).start()

            @pl.when(past == owned + 2)
            def _():
                gather_own()

            @pl.when(past == owned + 3)
            def _():
                spread_own()

    over(steps + max(OUTER, INNER), step)

    @pl.when(owned >= steps - 2)
    def _():
        gather_own()

    @pl.when(has_prior)
    def _():
        over(steps, lambda n: back_copy(n).start())

    @pl.when(owned >= steps - 3)
    def _():
        spread_own()

    def settle(n):
        @pl.when(has_next)
        def _():
            back_copy(n).wait_recv()

        packed[...] = back_in[n].astype(jnp.float32)
        for i in range(tiles):
            lanes = pl.ds(pl.multiple_of(n * chunk + i * LANES, LANES), LANES)
            for stream in range(3):
                tails[stream, 16 - margin : 16, lanes] += packed[spot(i, stream)]
                fixed = tails[stream, :, lanes].astype(jnp.bfloat16)
                results[n, 1 + stream, tokens - 16 : tokens, i * LANES : (i + 1) * LANES] = fixed
        for stream in range(3):
            save_tail(n, stream).start()

    def drain(n):
        for which in range(4):
            save(n, which).wait()
        for stream in range(3):
            save_tail(n, stream).wait()

        @pl.when(has_next)
        def _():
            head_copy(n).wait_send()
            u_copy(n, 0).wait_send()
            u_copy(n, 1).wait_send()
            u_copy(n, 2).wait_send()

        @pl.when(has_prior)
        def _():
            dz_copy(n, 0).wait_send()
            dz_copy(n, 1).wait_send()
            dz_copy(n, 2).wait_send()
            back_copy(n).wait_send()

    over(steps, settle)
    over(steps, drain)
    each(planes, place, lambda peer: first(peer, place).wait_send())
    each(depths, depth, lambda peer: second(peer, depth).wait_send())
    each(planes, place, lambda peer: third(peer, place).wait_send())
    each(planes, place, lambda peer: third(peer, peer).wait_recv())


def finish_kernel(
    mixed_in,
    query_in,
    key_in,
    value_in,
    sums_in,
    mixed,
    grad_query,
    grad_key,
    grad_value,
    short_out,
    filters_out,
    skip_out,
    sums,
    short,
    filters,
    skip,
    opened,
    stage,
    loaded,
    copied,
    other,
):
    pairs = (mixed_in, mixed), (query_in, grad_query), (key_in, grad_key), (value_in, grad_value)
    parts = copied.shape[1]
    half = mixed.shape[0] // parts
    loads, saves = [], []
    for index, (given, out) in enumerate(pairs):
        for part in range(parts):
            rows = pl.ds(part * half, half)
            here = stage.at[index, rows]
            loads.append(pltpu.make_async_copy(given.at[rows], here, loaded.at[index, part]))
            saves.append(pltpu.make_async_copy(here, out.at[rows], copied.at[index, part]))
    first = pltpu.make_async_copy(sums_in, sums, other.at[0])
    first.start()
    for copy in loads:
        copy.start()
    tiles = sums.shape[0]
    count_taps = short.shape[1]
    per_tile = filters.shape[0] // tiles
    square = (LANES, LANES)
    turn = lax.broadcasted_iota(jnp.int32, square, 0) + lax.broadcasted_iota(jnp.int32, square, 1)
    turn = jnp.where(turn == LANES - 1, 1.0, 0.0).astype(jnp.bfloat16)

    first.wait()
    for i in range(tiles):
        lanes = slice(i * LANES, (i + 1) * LANES)
        opened[i] = sums[i].astype(jnp.float32)
        for stream in range(3):
            short[stream, :, lanes] = opened[i, stream * 8 : stream * 8 + count_taps]
        skip[:, lanes] = opened[i, count_taps : count_taps + 1]
        filters[i * per_tile : (i + 1) * per_tile] = jnp.dot(
            opened[i, 24:].astype(jnp.bfloat16), turn, preferred_element_type=jnp.float32
        )
    pieces = ((short, short_out), (filters, filters_out), (skip, skip_out))
    for index, (given, out) in enumerate(pieces):
        saves.append(pltpu.make_async_copy(given, out, other.at[1 + index]))
        saves[-1].start()
    for coming, leaving in zip(loads, saves):
        coming.wait()
        leaving.start()
    for copy in saves:
        copy.wait()


def local_block(scale, query, keys, values, cotangent, taps, filters, skip, lengths):
    steps = STEPS
    tokens, width = query.shape
    groups = filters.shape[0]
    chunk = width // steps
    tiles = width // LANES
    count_taps = taps.shape[1]
    spots = -(-3 * (count_taps - 1) * (chunk // LANES) // 16) * 16
    bf16, f32 = jnp.bfloat16, jnp.float32
    stream = jax.ShapeDtypeStruct((tokens, width), bf16)
    vmem = pl.BlockSpec(memory_space=pltpu.VMEM)
    hbm = pl.BlockSpec(memory_space=pl.ANY)
    dma = pltpu.SemaphoreType.DMA((steps,))
    pair = pltpu.SemaphoreType.DMA((steps, 3))
    plane = pltpu.SemaphoreType.DMA((32,))
    depth = pltpu.SemaphoreType.DMA((8,))
    piece = pltpu.VMEM((steps, tokens, chunk), bf16)
    margin = pltpu.VMEM((steps, spots, LANES), bf16)
    made = pl.pallas_call(
        functools.partial(block_kernel, steps, width // groups, scale),
        out_shape=[stream] * 4
        + [jax.ShapeDtypeStruct((tiles, 32, LANES), bf16)],
        in_specs=[pl.BlockSpec(memory_space=pltpu.SMEM)] + [hbm] * 7,
        out_specs=[hbm] * 4 + [vmem],
        scratch_shapes=[
            pltpu.VMEM(taps.shape, f32),
            pltpu.VMEM(filters.shape, f32),
            pltpu.VMEM(skip.shape, f32),
            pltpu.SemaphoreType.DMA((3,)),
            pltpu.VMEM((steps, 4, tokens, chunk), bf16),
            pltpu.VMEM((steps, 4, tokens, chunk), bf16),
            pltpu.VMEM((3, 16, width), f32),
            pltpu.VMEM((tiles, 3, tokens + HALO, LANES), f32),
            pltpu.VMEM((tiles, 3, tokens, LANES), f32),
            pltpu.VMEM((groups, LANES), f32),
            piece,
            piece,
            piece,
            piece,
            margin,
            margin,
            margin,
            margin,
            pltpu.VMEM((chunk // LANES, 3, HALO, LANES), f32),
            pltpu.VMEM((spots, LANES), f32),
            pltpu.VMEM((tokens + 2 * HALO, LANES), jnp.int32),
            pltpu.VMEM((count_taps - 1, tokens, LANES), f32),
            pltpu.VMEM((count_taps, tokens + HALO, LANES), f32),
            pltpu.VMEM((tokens, 2 * tokens), bf16),
            pltpu.VMEM((tokens, 2 * tokens), f32),
            pltpu.VMEM((tokens, 2 * tokens), bf16),
            pltpu.VMEM((3, tokens + 2 * HALO, LANES), f32),
            pltpu.VMEM((32, LANES), f32),
            pltpu.VMEM((tiles, 32, LANES), bf16),
            pltpu.VMEM((32, 32, LANES), bf16),
            pltpu.VMEM((8, 32, LANES), bf16),
            pltpu.SemaphoreType.DMA((steps, 4)),
            pltpu.SemaphoreType.DMA((steps, 4)),
            pltpu.SemaphoreType.DMA((steps, 3)),
        ]
        + [pair] * 4
        + [dma] * 4
        + [plane, plane, depth, depth, plane, plane],
        compiler_params=pltpu.CompilerParams(
            collective_id=0, has_side_effects=True, vmem_limit_bytes=56 * 2**20
        ),
        name="block",
    )(lengths, query, keys, values, cotangent, taps, filters, skip)
    return pl.pallas_call(
        finish_kernel,
        out_shape=[stream] * 4
        + [
            jax.ShapeDtypeStruct(taps.shape, f32),
            jax.ShapeDtypeStruct(filters.shape, f32),
            jax.ShapeDtypeStruct(skip.shape, f32),
        ],
        in_specs=[hbm] * 5,
        out_specs=[hbm] * 7,
        scratch_shapes=[
            pltpu.VMEM((tiles, 32, LANES), bf16),
            pltpu.VMEM(taps.shape, f32),
            pltpu.VMEM(filters.shape, f32),
            pltpu.VMEM(skip.shape, f32),
            pltpu.VMEM((tiles, 32, LANES), f32),
            pltpu.VMEM((4, tokens, width), bf16),
            pltpu.SemaphoreType.DMA((4, 4)),
            pltpu.SemaphoreType.DMA((4, 4)),
            pltpu.SemaphoreType.DMA((4,)),
        ],
        compiler_params=pltpu.CompilerParams(vmem_limit_bytes=60 * 2**20),
        name="finish",
    )(*made)


def shards(
    query_proj, key_proj, value_proj, short_taps, filter_taps, skip_gain, doc_lengths, out_grad
):
    tokens = query_proj.shape[1]
    scale = 1.0 / math.sqrt(tokens * lax.axis_size("ctx") * lax.axis_size("dp"))
    mixed, grad_query, grad_key, grad_value, short, filters, gain = local_block(
        scale,
        query_proj[0],
        key_proj[0],
        value_proj[0],
        out_grad[0],
        short_taps,
        filter_taps,
        skip_gain[None],
        doc_lengths,
    )
    return (
        mixed[None],
        grad_query[None],
        grad_key[None],
        grad_value[None],
        short,
        filters,
        gain[0],
    )


def solution(mesh):
    return jax.shard_map(
        shards,
        mesh=mesh,
        in_specs=(
            P("dp", "ctx", None),
            P("dp", "ctx", None),
            P("dp", "ctx", None),
            P(),
            P(),
            P(),
            P("dp", None),
            P("dp", "ctx", None),
        ),
        out_specs=(
            P("dp", "ctx", None),
            P("dp", "ctx", None),
            P("dp", "ctx", None),
            P("dp", "ctx", None),
            P(),
            P(),
            P(),
        ),
        check_vma=False,
    )
```
